256 devices in a mesh: row: 2 (over x_lo), pass: 64 (over y, z, core), span: 2 (over x_hi).
Axes of the slice: x: 4 (x_hi: 2, x_lo: 2; x = x_hi * 2 + x_lo), y: 4, z: 8, core: 2. Of those that a mesh axis runs over, the one named last changes fastest.
Arguments:
- state: float32 [2, 5, 125, 1, 8, 8192], P('row', None, None, None, 'span', 'pass'), may hold values from -6 to 6
- old_state: float32 [2, 5, 125, 1, 8, 8192], P('row', None, None, None, 'span', 'pass'), may hold values from -6 to 6
- jacobians: float32 [3, 5, 5], replicated, may hold values from -2.5 to 2.5
- offset: int32 [1], replicated, may hold values from 0 to 8191
Outputs:
- residual: float32 [2, 5, 125, 1, 8, 8192], P('row', None, None, None, 'span', 'pass')
- correction: float32 [2, 5, 125, 1, 8, 8192], P('row', None, None, None, 'span', 'pass')
The draws below stay inside these ranges and needn't reach their ends.
Inputs may be any that keep to these rules, and one draw needn't show every extreme that they name: The offset is a whole number of pitchwise elements.
All inputs are finite; a program needn't handle non-finite values.
Results may differ from the reference program's by a relative error of at most 0.00011.
Values sent between devices are 32-bit elements; how exact they have to be, the bound alone decides.
A program may use at most 192 MiB of HBM per device.

```python
import math
import jax
import jax.numpy as jnp
import numpy as np
from jax import lax

VARS = 5
NODES = 125
EA = 1
SWEEPS = 3
NP = 8192
NS = 8


def steps_of(rng, dims, pieces, low, top_value):
    loudness = 1.0
    for axis_at, shards_of in pieces:
        heights = jax.random.uniform(jax.random.fold_in(jax.random.fold_in(rng, 6), axis_at), (shards_of,), jnp.float32, low / len(pieces), top_value / len(pieces))
        loudness = loudness * jnp.repeat(jnp.exp(heights), dims[axis_at] // shards_of).reshape((-1,) + (1,) * (len(dims) - 1 - axis_at))
    return loudness


def noise(stream_key, shape, scale, limit, split=(), held_as=jnp.bfloat16):
    values = jax.random.normal(stream_key, shape, jnp.float32) * scale
    if len(split) > 0:
        values = steps_of(stream_key, shape, split, -0.22, 0.18) * values
    return jnp.clip(values, min=-limit, max=limit).astype(held_as)


def setup_inputs(seed: int = 0) -> dict:
    streams_of = jax.random.split(jax.random.key(seed), 5)
    state = noise(streams_of[0], (2, VARS, NODES, EA, NS, NP), 1.0, 6.0, ((0, 2), (4, 2), (5, 64)), jnp.float32)
    old_state = noise(streams_of[1], (2, VARS, NODES, EA, NS, NP), 1.0, 6.0, ((0, 2), (4, 2), (5, 64)), jnp.float32)
    jacobians = noise(streams_of[2], (3, VARS, VARS), VARS ** -0.5, 2.5, (), jnp.float32)
    offset = jax.random.randint(streams_of[3], (1,), 0, NP).astype(jnp.int32)
    return dict(state=state, old_state=old_state, jacobians=jacobians, offset=offset)


LIFT_HALF = 5.0
INV_DT = 1.5
INV_DTAU = 1.0
DIAG = 12.0
OMEGA = 0.7

def gll_derivative():
    nodes = np.array([-1.0, -math.sqrt(3.0 / 7.0), 0.0, math.sqrt(3.0 / 7.0), 1.0])
    legend = (35.0 * nodes ** 4 - 30.0 * nodes ** 2 + 3.0) / 8.0
    table = np.zeros((5, 5))
    for left in range(5):
        for right in range(5):
            if left != right:
                table[left, right] = legend[left] / (legend[right] * (nodes[left] - nodes[right]))
    table[0, 0] = -5.0
    table[4, 4] = 5.0
    return jnp.asarray(table, jnp.float32)

def face_term(matrix, sign, jump):
    mixed = jnp.einsum('wv,v...->w...', matrix, jump, precision=lax.Precision.HIGHEST)
    return LIFT_HALF * (sign * mixed - jump)

def apply_op(padded, jacobians, lo_trace, hi_trace):
    highest = lax.Precision.HIGHEST
    deriv = gll_derivative()
    core = padded[..., 1:-1, 1:-1]
    grad_a = jnp.einsum('ij,vjbcxyz->vibcxyz', deriv, core, precision=highest)
    grad_p = jnp.einsum('ij,vajcxyz->vaicxyz', deriv, core, precision=highest)
    grad_s = jnp.einsum('ij,vabjxyz->vabixyz', deriv, core, precision=highest)
    result = jnp.einsum('wv,vabcxyz->wabcxyz', jacobians[0], grad_a, precision=highest)
    result = result + jnp.einsum('wv,vabcxyz->wabcxyz', jacobians[1], grad_p, precision=highest)
    result = result + jnp.einsum('wv,vabcxyz->wabcxyz', jacobians[2], grad_s, precision=highest)
    in_lo = core[:, 0]
    in_hi = core[:, 4]
    out_lo = jnp.concatenate([lo_trace[:, :, :, None], in_hi[:, :, :, :-1]], axis=3)
    out_hi = jnp.concatenate([in_lo[:, :, :, 1:], hi_trace[:, :, :, None]], axis=3)
    result = result.at[:, 0].add(face_term(jacobians[0], -1.0, out_lo - in_lo))
    result = result.at[:, 4].add(face_term(jacobians[0], 1.0, out_hi - in_hi))
    in_lo = core[:, :, 0]
    in_hi = core[:, :, 4]
    out_lo = padded[:, :, 4, :, :, 1:-1, :-2]
    out_hi = padded[:, :, 0, :, :, 1:-1, 2:]
    result = result.at[:, :, 0].add(face_term(jacobians[1], -1.0, out_lo - in_lo))
    result = result.at[:, :, 4].add(face_term(jacobians[1], 1.0, out_hi - in_hi))
    in_lo = core[:, :, :, 0]
    in_hi = core[:, :, :, 4]
    out_lo = padded[:, :, :, 4, :, :-2, 1:-1]
    out_hi = padded[:, :, :, 0, :, 2:, 1:-1]
    result = result.at[:, :, :, 0].add(face_term(jacobians[2], -1.0, out_lo - in_lo))
    result = result.at[:, :, :, 4].add(face_term(jacobians[2], 1.0, out_hi - in_hi))
    return result

def pad_row(field):
    wrapped = jnp.concatenate([field[..., -1:], field, field[..., :1]], axis=6)
    return jnp.pad(wrapped, [(0, 0)] * 5 + [(1, 1), (0, 0)])

def reference(state, old_state, jacobians, offset):
    shape = (2, 5, 5, 5, 5, EA, NS, NP)
    fields = state.reshape(shape)
    olds = old_state.reshape(shape)
    amount = offset[0] % NP
    rotor_face = fields[0][:, 4, :, :, EA - 1]
    stator_face = fields[1][:, 0, :, :, 0]
    rotor_hi = jnp.roll(stator_face, -amount, axis=4)
    stator_lo = jnp.roll(rotor_face, amount, axis=4)
    blank = jnp.zeros_like(rotor_face)
    bounds = ((blank, rotor_hi), (stator_lo, blank))
    residuals = []
    corrections = []
    for which in range(2):
        field = fields[which]
        lower, upper = bounds[which]
        residual = (field - olds[which]) * INV_DT + apply_op(pad_row(field), jacobians, lower, upper)
        update = -residual / DIAG
        for sweep in range(SWEEPS):
            image = (INV_DT + INV_DTAU) * update + apply_op(pad_row(update), jacobians, blank, blank)
            update = update - OMEGA / DIAG * (residual + image)
        residuals.append(residual)
        corrections.append(update)
    final = (2, 5, 125, EA, NS, NP)
    return (jnp.stack(residuals).reshape(final), jnp.stack(corrections).reshape(final))
```

```python
import functools
import math

import jax
import jax.numpy as jnp
import numpy as np
from jax import lax
from jax.experimental import pallas as pl
from jax.experimental.pallas import tpu as pltpu
from jax.sharding import PartitionSpec as P

SWEEPS = 3
LIFT_HALF = 5.0
INV_DT = 1.5
INV_DTAU = 1.0
DIAG = 12.0
OMEGA = 0.7

LANES = 128
SLICE = 128
SLICES = 20
TRACE = 512
MESH = pl.DeviceIdType.MESH
HIGHEST = lax.Precision.HIGHEST


def gll_derivative():
    nodes = np.array([-1.0, -math.sqrt(3.0 / 7.0), 0.0, math.sqrt(3.0 / 7.0), 1.0])
    legend = (35.0 * nodes**4 - 30.0 * nodes**2 + 3.0) / 8.0
    table = np.zeros((5, 5))
    for left in range(5):
        for right in range(5):
            if left != right:
                table[left, right] = legend[left] / (legend[right] * (nodes[left] - nodes[right]))
    return table


def operator_patterns():
    deriv = gll_derivative()
    planes = np.zeros((13, SLICE, SLICE), np.float32)
    places = [(v, a, p) for v in range(5) for a in range(5) for p in range(5)]
    for q, (v, a, p) in enumerate(places):
        planes[12, q, v] = 1.0
        planes[4, v, q] = 1.0
        planes[3, q, q] = LIFT_HALF * ((a in (0, 4)) + (p in (0, 4)))
        for c, (w, b, r) in enumerate(places):
            planes[0, q, c] = deriv[a, b] * (p == r)
            planes[1, q, c] = deriv[p, r] * (a == b)
            planes[2, q, c] = (a == b) * (p == r)
        for w in range(5):
            for k in range(5):
                low, high, face = 5 * w + k, 32 + 5 * w + k, 64 + 5 * w + k
                if p == 0 and a == k:
                    planes[7, q, low] = -LIFT_HALF
                    planes[8:10, q, low] = -LIFT_HALF * (v == w)
                if p == 4 and a == k:
                    planes[7, q, high] = LIFT_HALF
                    planes[8:10, q, high] = -LIFT_HALF * (v == w)
                if a == 4 and p == k:
                    planes[10, q, face] = LIFT_HALF
                    planes[8, q, face] = -LIFT_HALF * (v == w)
                if a == 0 and p == k:
                    planes[11, q, face] = -LIFT_HALF
                    planes[9, q, face] = -LIFT_HALF * (v == w)
    for w in range(5):
        planes[5, w, 5 * w : 5 * w + 5] = 1.0
        planes[5, w, 32 + 5 * w : 32 + 5 * w + 5] = 1.0
        planes[6, w, 64 + 5 * w : 64 + 5 * w + 5] = 1.0
    return planes


def halves(x):
    high = x.astype(jnp.bfloat16)
    low = (x - high.astype(jnp.float32)).astype(jnp.bfloat16)
    return high, low


def kernel(
    passes,
    state, older, jacobians, offset, planes,
    residual_out, update_out,
    values, resid, trace, turned, ready, facing, pats, spread,
    main_op, ghost_op, face_op, main_x, ghost_x, face_x,
    pack_up, pack_down, from_low, from_high, from_span,
    load_sem, old_sem, trace_sem, pat_sem, out_sem,
    turn_send, turn_recv, face_send, face_recv, halo_send, halo_recv,
):
    row, here, span = lax.axis_index("row"), lax.axis_index("pass"), lax.axis_index("span")
    up, down = lax.rem(here + 1, passes), lax.rem(here + passes - 1, passes)
    tile = TRACE // passes
    deriv = gll_derivative()

    loads = [
        pltpu.make_async_copy(state.at[:, j, 0, :], values.at[0, pl.ds(SLICE * j, 125)], load_sem.at[j])
        for j in range(SLICES)
    ]
    old_loads = [
        pltpu.make_async_copy(older.at[:, j, 0, :], resid.at[j, pl.ds(0, 125)], old_sem.at[j])
        for j in range(SLICES)
    ]
    plane_at = 20 * (1 - row)
    trace_loads = [
        pltpu.make_async_copy(
            state.at[pl.ds(25 * v + plane_at, 5)], trace.at[pl.ds(5 * v, 5)], trace_sem.at[v]
        )
        for v in range(5)
    ]
    pat_load = pltpu.make_async_copy(planes, pats, pat_sem)
    for copy in trace_loads + loads + [pat_load] + old_loads:
        copy.start()

    barrier = pltpu.get_barrier_semaphore()

    def greet(step, carry):
        other = lax.rem(here + step, passes)
        pl.semaphore_signal(barrier, inc=1, device_id=(row, other, span), device_id_type=MESH)
        pl.semaphore_signal(barrier, inc=1, device_id=(1 - row, other, span), device_id_type=MESH)
        return carry

    pl.semaphore_signal(barrier, inc=1, device_id=(row, here, 1 - span), device_id_type=MESH)
    pl.semaphore_signal(barrier, inc=1, device_id=(1 - row, here, span), device_id_type=MESH)
    lax.fori_loop(1, passes, greet, 0)

    for slot in range(2):
        for j in range(SLICES):
            values[slot, pl.ds(SLICE * j + 125, 3), :] = jnp.zeros((3, LANES), jnp.float32)
        values[slot, pl.ds(SLICE * SLICES, 40), :] = jnp.zeros((40, LANES), jnp.float32)
    for j in range(SLICES):
        resid[j, pl.ds(125, 3), :] = jnp.zeros((3, LANES), jnp.float32)
    trace[pl.ds(25, 1)] = jnp.zeros((1, SLICES, 1, LANES), jnp.float32)

    pat_load.wait()
    spread[...] = jnp.zeros_like(spread)
    for d in range(3):
        spread[d, 0:5, 0:5] = jacobians[:, d, :]
    rows = pats[12][:, 0:8]

    def spread_out(d, plane):
        by_row = jnp.dot(rows, spread[d], precision=HIGHEST, preferred_element_type=jnp.float32)
        return jnp.dot(by_row, pats[plane], precision=HIGHEST, preferred_element_type=jnp.float32)

    own = spread_out(0, 4) * pats[0] + spread_out(1, 4) * pats[1] + pats[3]
    along = spread_out(2, 4) * pats[2]
    edges = spread_out(1, 5) * pats[7] + spread_out(0, 6) * pats[10 + row] + pats[8 + row]
    for part, block in enumerate((own, along)):
        for half, piece in enumerate(halves(block)):
            for again in range(2):
                main_op[pl.ds(SLICE * half, SLICE), pl.ds(2 * SLICE * again + SLICE * part, SLICE)] = piece
    for half, piece in enumerate(halves(edges)):
        for again in range(2):
            ghost_op[pl.ds(SLICE * half, SLICE), pl.ds(64 * again, 64)] = piece[:, 0:64]
            face_op[pl.ds(SLICE * half, SLICE), pl.ds(32 * again, 32)] = piece[:, 64:96]

    lane = lax.broadcasted_iota(jnp.int32, (32, LANES), 1)

    def pitch_rows(slot, j, node):
        return values[slot, pl.ds(SLICE * j + node, 32, stride=5), :]

    def halo_copies(slot, t):
        sent = SLICE * (SLICES - 1) * (1 - span)
        return [
            pltpu.make_async_remote_copy(
                src_ref=values.at[slot, pl.ds(pl.multiple_of(sent, SLICE), SLICE)], dst_ref=from_span.at[t],
                send_sem=halo_send.at[0, t], recv_sem=halo_recv.at[0, t],
                device_id=(row, here, 1 - span), device_id_type=MESH),
            pltpu.make_async_remote_copy(
                src_ref=pack_up.at[t], dst_ref=from_low.at[t],
                send_sem=halo_send.at[1, t], recv_sem=halo_recv.at[1, t],
                device_id=(row, up, span), device_id_type=MESH),
            pltpu.make_async_remote_copy(
                src_ref=pack_down.at[t], dst_ref=from_high.at[t],
                send_sem=halo_send.at[2, t], recv_sem=halo_recv.at[2, t],
                device_id=(row, down, span), device_id_type=MESH),
        ]

    def start_halo(slot, t):
        copies = halo_copies(slot, t)
        copies[0].start()
        upward = jnp.zeros((32, LANES), jnp.float32)
        downward = jnp.zeros((32, LANES), jnp.float32)
        for j in range(SLICES):
            upward = jnp.where(lane == j, pltpu.roll(pitch_rows(slot, j, 4), j + 1, 1), upward)
            first = pitch_rows(slot, j, 0)
            downward = jnp.where(lane == j, pltpu.roll(first, j, 1) if j else first, downward)
        pack_up[t] = upward
        pack_down[t] = downward
        copies[1].start()
        copies[2].start()

    def wait_halo(slot, t):
        for copy in halo_copies(slot, t):
            copy.wait()

    def span_ghost(slot, t, elem, low, at, size):
        if low and elem > 0:
            return values[slot, pl.ds(SLICE * (16 + elem - 1) + at, size), :]
        if not low and elem < 3:
            return values[slot, pl.ds(SLICE * (elem + 1) + at, size), :]
        got = from_span[t, pl.ds(at, size), :]
        return jnp.where(span == (1 if low else 0), got, jnp.zeros_like(got))

    def split_main(slot, t, elem):
        cols = pl.ds(LANES * elem, LANES)

        def chunk(c, carry):
            at = pl.multiple_of(16 * c, 16)
            v = [values[slot, pl.ds(pl.multiple_of(SLICE * (4 * s + elem) + at, 16), 16), :] for s in range(5)]
            low = span_ghost(slot, t, elem, True, at, 16)
            high = span_ghost(slot, t, elem, False, at, 16)
            sum04, dif04, sum13, dif13 = v[0] + v[4], v[0] - v[4], v[1] + v[3], v[1] - v[3]
            d = lambda i, j: float(deriv[i, j])
            odd0 = (0.5 * (d(0, 1) + d(0, 3))) * sum13 + d(0, 2) * v[2] + (0.5 * d(0, 4)) * sum04
            even0 = (0.5 * (d(0, 1) - d(0, 3))) * dif13 - (0.5 * d(0, 4)) * dif04
            odd1 = (0.5 * (d(1, 0) + d(1, 4))) * sum04 + d(1, 2) * v[2] + (0.5 * d(1, 3)) * sum13
            even1 = (0.5 * (d(1, 0) - d(1, 4))) * dif04 - (0.5 * d(1, 3)) * dif13
            g = [
                even0 + odd0 - LIFT_HALF * low,
                even1 + odd1,
                d(2, 0) * dif04 + d(2, 1) * dif13,
                even1 - odd1,
                even0 - odd0 + LIFT_HALF * high,
            ]
            for s in range(5):
                for part, block in enumerate((v[s], g[s])):
                    for half, piece in enumerate(halves(block)):
                        place = 2 * SLICE * half + SLICE * part
                        main_x[s, pl.ds(pl.multiple_of(place + at, 16), 16), cols] = piece
            return carry

        lax.fori_loop(0, SLICE // 16, chunk, 0)

    def split_ghosts(slot, t):
        lows, highs = from_low[t], from_high[t]
        for j in range(SLICES):
            cols = pl.ds(LANES * (j % 4), LANES)
            got = pltpu.roll(lows, LANES - j, 1) if j else lows
            low = jnp.where(lane == 0, got, pltpu.roll(pitch_rows(slot, j, 4), 1, 1))
            got = pltpu.roll(highs, LANES - 1 - j, 1)
            high = jnp.where(lane == LANES - 1, got, pltpu.roll(pitch_rows(slot, j, 0), LANES - 1, 1))
            for part, block in enumerate((low, high)):
                for half, piece in enumerate(halves(block)):
                    ghost_x[j // 4, pl.ds(64 * half + 32 * part, 32), cols] = piece

    def apply(slot, t, store):
        for s in range(5):
            image = jnp.dot(main_op[...], main_x[s], preferred_element_type=jnp.float32)
            image = image + jnp.dot(ghost_op[...], ghost_x[s], preferred_element_type=jnp.float32)
            image = image[0:SLICE] + image[SLICE : 2 * SLICE]
            for elem in range(4):
                j = 4 * s + elem
                mine = values[slot, pl.ds(SLICE * j, SLICE), :]
                part = image[:, LANES * elem : LANES * (elem + 1)]
                if s in (0, 4):
                    part = part + LIFT_HALF * (mine - span_ghost(slot, t, elem, s == 0, 0, SLICE))
                store(j, mine, part)

    for copy in trace_loads:
        copy.wait()
    pl.semaphore_wait(barrier, 2 * passes)
    flat = trace.reshape(26 * SLICES, LANES)

    def turn_copy(other):
        return pltpu.make_async_remote_copy(
            src_ref=flat.at[pl.ds(pl.multiple_of(tile * other, tile), tile)], dst_ref=turned.at[here],
            send_sem=turn_send, recv_sem=turn_recv, device_id=(row, other, span), device_id_type=MESH)

    def turn(step, carry):
        turn_copy(lax.rem(here + step, passes)).start()
        return carry

    lax.fori_loop(1, passes, turn, 0)
    turned[here] = flat[pl.ds(pl.multiple_of(tile * here, tile), tile), :]

    for copy in loads:
        copy.wait()
    start_halo(0, 0)
    for elem in (1, 2):
        split_main(0, 0, elem)

    all_turned = pltpu.make_async_remote_copy(
        src_ref=turned.at[pl.ds(0, passes - 1)], dst_ref=turned.at[pl.ds(0, passes - 1)],
        send_sem=turn_send, recv_sem=turn_recv, device_id=(row, up, span), device_id_type=MESH)
    all_turned.wait()
    total = LANES * passes
    shift = lax.rem(lax.rem(offset[0], total) + total, total)
    shift = jnp.where(row == 0, shift, lax.rem(total - shift, total))
    places = shift // LANES
    within = lax.rem(shift, LANES)
    tile_lane = lax.broadcasted_iota(jnp.int32, (tile, LANES), 1)

    def rotate(other, carry):
        near = turned[lax.rem(other - places + passes, passes)]
        far = turned[lax.rem(other - places + 2 * passes - 1, passes)]
        ready[other] = pltpu.roll(jnp.where(tile_lane < LANES - within, near, far), within, 1)
        return carry

    lax.fori_loop(0, passes, rotate, 0)

    def face_copy(other):
        return pltpu.make_async_remote_copy(
            src_ref=ready.at[other], dst_ref=facing.at[pl.ds(pl.multiple_of(tile * here, tile), tile)],
            send_sem=face_send, recv_sem=face_recv, device_id=(1 - row, other, span), device_id_type=MESH)

    def send_face(step, carry):
        face_copy(lax.rem(here + step, passes)).start()
        return carry

    lax.fori_loop(0, passes, send_face, 0)

    wait_halo(0, 0)
    for elem in (0, 3):
        split_main(0, 0, elem)
    split_ghosts(0, 0)
    for copy in old_loads:
        copy.wait()

    def store_residual(j, mine, part):
        resid[j] = INV_DT * (mine - resid[j]) + part

    apply(0, 0, store_residual)

    all_faced = pltpu.make_async_remote_copy(
        src_ref=facing, dst_ref=facing, send_sem=face_send, recv_sem=face_recv,
        device_id=(1 - row, here, span), device_id_type=MESH)
    all_faced.wait()

    for j in range(SLICES):
        block = facing[pl.ds(j, 25, stride=SLICES), :]
        block = jnp.concatenate([block, jnp.zeros((7, LANES), jnp.float32)], axis=0)
        for half, piece in enumerate(halves(block)):
            face_x[j // 4, pl.ds(32 * half, 32), pl.ds(LANES * (j % 4), LANES)] = piece
    outs = [
        pltpu.make_async_copy(resid.at[j, pl.ds(0, 125)], residual_out.at[:, j, 0, :], out_sem.at[0, j])
        for j in range(SLICES)
    ]
    for s in range(5):
        image = jnp.dot(face_op[...], face_x[s], preferred_element_type=jnp.float32)
        image = image[0:SLICE] + image[SLICE : 2 * SLICE]
        for elem in range(4):
            j = 4 * s + elem
            whole = resid[j] + image[:, LANES * elem : LANES * (elem + 1)]
            resid[j] = whole
            values[1, pl.ds(SLICE * j, SLICE), :] = whole * (-1.0 / DIAG)
    for copy in outs:
        copy.start()

    rate = OMEGA / DIAG

    def sweep(t, carry):
        slot = lax.rem(t, 2)
        start_halo(slot, t)
        for elem in (1, 2):
            split_main(slot, t, elem)
        wait_halo(slot, t)
        for elem in (0, 3):
            split_main(slot, t, elem)
        split_ghosts(slot, t)

        def store(j, mine, part):
            image = (INV_DT + INV_DTAU) * mine + part
            values[1 - slot, pl.ds(SLICE * j, SLICE), :] = mine - rate * (resid[j] + image)

        apply(slot, t, store)
        return carry

    lax.fori_loop(1, SWEEPS + 1, sweep, 0)

    last = (SWEEPS + 1) % 2
    final = [
        pltpu.make_async_copy(
            values.at[last, pl.ds(SLICE * j, 125)], update_out.at[:, j, 0, :], out_sem.at[1, j]
        )
        for j in range(SLICES)
    ]
    for copy in final:
        copy.start()
    for copy in outs + final:
        copy.wait()


def per_device(passes, state, old_state, jacobians, offset):
    shape = state.shape
    tile = TRACE // passes
    anywhere = pl.BlockSpec(memory_space=pl.ANY)
    f32, bf16, dma = jnp.float32, jnp.bfloat16, pltpu.SemaphoreType.DMA
    exchanges = SWEEPS + 1
    viewed = (125, SLICES, 1, LANES)
    outs = pl.pallas_call(
        functools.partial(kernel, passes),
        out_shape=[jax.ShapeDtypeStruct(viewed, f32)] * 2,
        in_specs=[anywhere, anywhere, pl.BlockSpec(memory_space=pltpu.VMEM),
                  pl.BlockSpec(memory_space=pltpu.SMEM), anywhere],
        out_specs=[anywhere] * 2,
        scratch_shapes=[
            pltpu.VMEM((2, SLICE * SLICES + 40, LANES), f32),
            pltpu.VMEM((SLICES, SLICE, LANES), f32),
            pltpu.VMEM((26, SLICES, 1, LANES), f32),
            pltpu.VMEM((passes, tile, LANES), f32),
            pltpu.VMEM((passes, tile, LANES), f32),
            pltpu.VMEM((TRACE, LANES), f32),
            pltpu.VMEM((13, SLICE, SLICE), f32),
            pltpu.VMEM((3, 8, LANES), f32),
            pltpu.VMEM((2 * SLICE, 4 * SLICE), bf16),
            pltpu.VMEM((2 * SLICE, 128), bf16),
            pltpu.VMEM((2 * SLICE, 64), bf16),
            pltpu.VMEM((5, 4 * SLICE, 4 * LANES), bf16),
            pltpu.VMEM((5, 128, 4 * LANES), bf16),
            pltpu.VMEM((5, 64, 4 * LANES), bf16),
            pltpu.VMEM((exchanges, 32, LANES), f32),
            pltpu.VMEM((exchanges, 32, LANES), f32),
            pltpu.VMEM((exchanges, 32, LANES), f32),
            pltpu.VMEM((exchanges, 32, LANES), f32),
            pltpu.VMEM((exchanges, SLICE, LANES), f32),
            dma((SLICES,)), dma((SLICES,)), dma((5,)), dma, dma((2, SLICES)),
            dma, dma, dma, dma, dma((3, exchanges)), dma((3, exchanges)),
        ],
        compiler_params=pltpu.CompilerParams(
            collective_id=0, has_side_effects=True, vmem_limit_bytes=48 * 1024 * 1024
        ),
        name="pseudo_step",
    )(
        state.reshape(viewed), old_state.reshape(viewed),
        jnp.transpose(jacobians, (1, 0, 2)), offset, operator_patterns(),
    )
    return tuple(out.reshape(shape) for out in outs)


def solution(mesh):
    placed = P("row", None, None, None, "span", "pass")
    return jax.shard_map(
        functools.partial(per_device, mesh.shape["pass"]),
        mesh=mesh,
        in_specs=(placed, placed, P(), P()),
        out_specs=(placed, placed),
        check_vma=False,
    )
```

```python
import functools
import math

import jax
import jax.numpy as jnp
import numpy as np
from jax import lax
from jax.experimental import pallas as pl
from jax.experimental.pallas import tpu as pltpu
from jax.sharding import PartitionSpec as P

SWEEPS = 3
LIFT_HALF = 5.0
INV_DT = 1.5
INV_DTAU = 1.0
DIAG = 12.0
OMEGA = 0.7

LANES = 128
SLICE = 128
SLICES = 20
TRACE = 512
MESH = pl.DeviceIdType.MESH
HIGHEST = lax.Precision.HIGHEST


def gll_derivative():
    nodes = np.array([-1.0, -math.sqrt(3.0 / 7.0), 0.0, math.sqrt(3.0 / 7.0), 1.0])
    legend = (35.0 * nodes**4 - 30.0 * nodes**2 + 3.0) / 8.0
    table = np.zeros((5, 5))
    for left in range(5):
        for right in range(5):
            if left != right:
                table[left, right] = legend[left] / (legend[right] * (nodes[left] - nodes[right]))
    return table


def operator_patterns():
    deriv = gll_derivative()
    planes = np.zeros((13, SLICE, SLICE), np.float32)
    places = [(v, a, p) for v in range(5) for a in range(5) for p in range(5)]
    for q, (v, a, p) in enumerate(places):
        planes[12, q, v] = 1.0
        planes[4, v, q] = 1.0
        planes[3, q, q] = LIFT_HALF * ((a in (0, 4)) + (p in (0, 4)))
        for c, (w, b, r) in enumerate(places):
            planes[0, q, c] = deriv[a, b] * (p == r)
            planes[1, q, c] = deriv[p, r] * (a == b)
            planes[2, q, c] = (a == b) * (p == r)
        for w in range(5):
            for k in range(5):
                low, high, face = 5 * w + k, 32 + 5 * w + k, 64 + 5 * w + k
                if p == 0 and a == k:
                    planes[7, q, low] = -LIFT_HALF
                    planes[8:10, q, low] = -LIFT_HALF * (v == w)
                if p == 4 and a == k:
                    planes[7, q, high] = LIFT_HALF
                    planes[8:10, q, high] = -LIFT_HALF * (v == w)
                if a == 4 and p == k:
                    planes[10, q, face] = LIFT_HALF
                    planes[8, q, face] = -LIFT_HALF * (v == w)
                if a == 0 and p == k:
                    planes[11, q, face] = -LIFT_HALF
                    planes[9, q, face] = -LIFT_HALF * (v == w)
    for w in range(5):
        planes[5, w, 5 * w : 5 * w + 5] = 1.0
        planes[5, w, 32 + 5 * w : 32 + 5 * w + 5] = 1.0
        planes[6, w, 64 + 5 * w : 64 + 5 * w + 5] = 1.0
    return planes


def halves(x):
    high = x.astype(jnp.bfloat16)
    low = (x - high.astype(jnp.float32)).astype(jnp.bfloat16)
    return high, low


def kernel(
    passes,
    state, older, jacobians, offset, planes,
    residual_out, update_out,
    values, resid, trace, turned, ready, facing, pats, spread,
    jacs, main_op, ghost_op, face_op, main_x, ghost_x, face_x,
    pack_up, pack_down, from_low, from_high, from_span,
    load_sem, old_sem, trace_sem, pat_sem, jac_sem, out_sem,
    turn_send, turn_recv, face_send, face_recv, halo_send, halo_recv,
):
    row, here, span = lax.axis_index("row"), lax.axis_index("pass"), lax.axis_index("span")
    up, down = lax.rem(here + 1, passes), lax.rem(here + passes - 1, passes)
    tile = TRACE // passes
    deriv = gll_derivative()

    def peer(step):
        turn_z, turn_y, turn_core = step // 8, lax.rem(step // 2, 4), lax.rem(step + 1, 2)
        along_z = 4 + (1 - 2 * lax.rem(turn_z, 2)) * ((turn_z + 1) // 2)
        along_y = 2 + (1 - 2 * lax.rem(turn_y, 2)) * ((turn_y + 1) // 2)
        y = lax.rem(here // 16 + along_y, 4)
        z = lax.rem(here // 2 + along_z, 8)
        return 16 * y + 2 * z + lax.rem(here + turn_core, 2)

    barrier = pltpu.get_barrier_semaphore()

    def greet(step, carry):
        other = peer(step)
        pl.semaphore_signal(barrier, inc=1, device_id=(1 - row, other, span), device_id_type=MESH)
        pl.semaphore_signal(barrier, inc=1, device_id=(row, other, span), device_id_type=MESH)
        return carry

    lax.fori_loop(0, passes - 1, greet, 0)
    pl.semaphore_signal(barrier, inc=1, device_id=(1 - row, here, span), device_id_type=MESH)
    pl.semaphore_signal(barrier, inc=1, device_id=(row, here, 1 - span), device_id_type=MESH)

    loads = [
        pltpu.make_async_copy(state.at[:, j, 0, :], values.at[0, pl.ds(SLICE * j, 125)], load_sem.at[j])
        for j in range(SLICES)
    ]
    old_loads = [
        pltpu.make_async_copy(older.at[:, j, 0, :], resid.at[j, pl.ds(0, 125)], old_sem.at[j])
        for j in range(SLICES)
    ]
    plane_at = 20 * (1 - row)
    trace_loads = [
        pltpu.make_async_copy(
            state.at[pl.ds(25 * v + plane_at, 5)], trace.at[pl.ds(5 * v, 5)], trace_sem.at[v]
        )
        for v in range(5)
    ]
    pat_load = pltpu.make_async_copy(planes, pats, pat_sem)
    jac_load = pltpu.make_async_copy(jacobians, jacs, jac_sem)
    for copy in trace_loads + loads + [pat_load, jac_load] + old_loads:
        copy.start()

    lane = lax.broadcasted_iota(jnp.int32, (32, LANES), 1)

    def pitch_rows(slot, j, node):
        return values[slot, pl.ds(SLICE * j + node, 32, stride=5), :]

    def halo_copies(slot, t):
        sent = SLICE * (SLICES - 1) * (1 - span)
        return [
            pltpu.make_async_remote_copy(
                src_ref=values.at[slot, pl.ds(pl.multiple_of(sent, SLICE), SLICE)], dst_ref=from_span.at[t],
                send_sem=halo_send.at[0, t], recv_sem=halo_recv.at[0, t],
                device_id=(row, here, 1 - span), device_id_type=MESH),
            pltpu.make_async_remote_copy(
                src_ref=pack_up.at[t], dst_ref=from_low.at[t],
                send_sem=halo_send.at[1, t], recv_sem=halo_recv.at[1, t],
                device_id=(row, up, span), device_id_type=MESH),
            pltpu.make_async_remote_copy(
                src_ref=pack_down.at[t], dst_ref=from_high.at[t],
                send_sem=halo_send.at[2, t], recv_sem=halo_recv.at[2, t],
                device_id=(row, down, span), device_id_type=MESH),
        ]

    def start_halo(slot, t):
        copies = halo_copies(slot, t)
        copies[0].start()
        upward = jnp.zeros((32, LANES), jnp.float32)
        downward = jnp.zeros((32, LANES), jnp.float32)
        for j in range(SLICES):
            upward = jnp.where(lane == j, pltpu.roll(pitch_rows(slot, j, 4), j + 1, 1), upward)
            first = pitch_rows(slot, j, 0)
            downward = jnp.where(lane == j, pltpu.roll(first, j, 1) if j else first, downward)
        pack_up[t] = upward
        pack_down[t] = downward
        copies[1].start()
        copies[2].start()

    def wait_halo(slot, t):
        for copy in halo_copies(slot, t):
            copy.wait()

    def span_ghost(slot, t, elem, low, at, size):
        if low and elem > 0:
            return values[slot, pl.ds(SLICE * (16 + elem - 1) + at, size), :]
        if not low and elem < 3:
            return values[slot, pl.ds(SLICE * (elem + 1) + at, size), :]
        got = from_span[t, pl.ds(at, size), :]
        return jnp.where(span == (1 if low else 0), got, jnp.zeros_like(got))

    def split_main(slot, t, elem):
        cols = pl.ds(LANES * elem, LANES)

        def chunk(c, carry):
            at = pl.multiple_of(16 * c, 16)
            v = [values[slot, pl.ds(pl.multiple_of(SLICE * (4 * s + elem) + at, 16), 16), :] for s in range(5)]
            low = span_ghost(slot, t, elem, True, at, 16)
            high = span_ghost(slot, t, elem, False, at, 16)
            sum04, dif04, sum13, dif13 = v[0] + v[4], v[0] - v[4], v[1] + v[3], v[1] - v[3]
            d = lambda i, j: float(deriv[i, j])
            odd0 = (0.5 * (d(0, 1) + d(0, 3))) * sum13 + d(0, 2) * v[2] + (0.5 * d(0, 4)) * sum04
            even0 = (0.5 * (d(0, 1) - d(0, 3))) * dif13 - (0.5 * d(0, 4)) * dif04
            odd1 = (0.5 * (d(1, 0) + d(1, 4))) * sum04 + d(1, 2) * v[2] + (0.5 * d(1, 3)) * sum13
            even1 = (0.5 * (d(1, 0) - d(1, 4))) * dif04 - (0.5 * d(1, 3)) * dif13
            g = [
                even0 + odd0 - LIFT_HALF * low,
                even1 + odd1,
                d(2, 0) * dif04 + d(2, 1) * dif13,
                even1 - odd1,
                even0 - odd0 + LIFT_HALF * high,
            ]
            for s in range(5):
                for part, block in enumerate((v[s], g[s])):
                    for half, piece in enumerate(halves(block)):
                        place = 2 * SLICE * half + SLICE * part
                        main_x[s, pl.ds(pl.multiple_of(place + at, 16), 16), cols] = piece
            return carry

        lax.fori_loop(0, SLICE // 16, chunk, 0)

    def split_ghosts(slot, t):
        lows, highs = from_low[t], from_high[t]
        for j in range(SLICES):
            cols = pl.ds(LANES * (j % 4), LANES)
            got = pltpu.roll(lows, LANES - j, 1) if j else lows
            low = jnp.where(lane == 0, got, pltpu.roll(pitch_rows(slot, j, 4), 1, 1))
            got = pltpu.roll(highs, LANES - 1 - j, 1)
            high = jnp.where(lane == LANES - 1, got, pltpu.roll(pitch_rows(slot, j, 0), LANES - 1, 1))
            for part, block in enumerate((low, high)):
                for half, piece in enumerate(halves(block)):
                    ghost_x[j // 4, pl.ds(64 * half + 32 * part, 32), cols] = piece

    def apply(slot, t, store):
        for s in range(5):
            image = jnp.dot(main_op[...], main_x[s], preferred_element_type=jnp.float32)
            image = image + jnp.dot(ghost_op[...], ghost_x[s], preferred_element_type=jnp.float32)
            image = image[0:SLICE] + image[SLICE : 2 * SLICE]
            for elem in range(4):
                j = 4 * s + elem
                mine = values[slot, pl.ds(SLICE * j, SLICE), :]
                part = image[:, LANES * elem : LANES * (elem + 1)]
                if s in (0, 4):
                    part = part + LIFT_HALF * (mine - span_ghost(slot, t, elem, s == 0, 0, SLICE))
                store(j, mine, part)

    trace[pl.ds(25, 1)] = jnp.zeros((1, SLICES, 1, LANES), jnp.float32)
    for copy in trace_loads:
        copy.wait()
    pl.semaphore_wait(barrier, 2 * passes)
    flat = trace.reshape(26 * SLICES, LANES)

    def turn_copy(other):
        return pltpu.make_async_remote_copy(
            src_ref=flat.at[pl.ds(pl.multiple_of(tile * other, tile), tile)], dst_ref=turned.at[here],
            send_sem=turn_send, recv_sem=turn_recv, device_id=(row, other, span), device_id_type=MESH)

    def turn(step, carry):
        turn_copy(peer(step)).start()
        return carry

    lax.fori_loop(0, passes - 1, turn, 0)
    turned[here] = flat[pl.ds(pl.multiple_of(tile * here, tile), tile), :]

    for slot in range(2):
        for j in range(SLICES):
            values[slot, pl.ds(SLICE * j + 125, 3), :] = jnp.zeros((3, LANES), jnp.float32)
        values[slot, pl.ds(SLICE * SLICES, 40), :] = jnp.zeros((40, LANES), jnp.float32)
    for j in range(SLICES):
        resid[j, pl.ds(125, 3), :] = jnp.zeros((3, LANES), jnp.float32)

    pat_load.wait()
    jac_load.wait()
    spread[...] = jnp.zeros_like(spread)
    for d in range(3):
        spread[d, 0:5, 0:5] = jacs[:, d, :]
    rows = pats[12][:, 0:8]

    def spread_out(d, plane):
        by_row = jnp.dot(rows, spread[d], precision=HIGHEST, preferred_element_type=jnp.float32)
        return jnp.dot(by_row, pats[plane], precision=HIGHEST, preferred_element_type=jnp.float32)

    own = spread_out(0, 4) * pats[0] + spread_out(1, 4) * pats[1] + pats[3]
    along = spread_out(2, 4) * pats[2]
    edges = spread_out(1, 5) * pats[7] + spread_out(0, 6) * pats[10 + row] + pats[8 + row]
    for part, block in enumerate((own, along)):
        for half, piece in enumerate(halves(block)):
            for again in range(2):
                main_op[pl.ds(SLICE * half, SLICE), pl.ds(2 * SLICE * again + SLICE * part, SLICE)] = piece
    for half, piece in enumerate(halves(edges)):
        for again in range(2):
            ghost_op[pl.ds(SLICE * half, SLICE), pl.ds(64 * again, 64)] = piece[:, 0:64]
            face_op[pl.ds(SLICE * half, SLICE), pl.ds(32 * again, 32)] = piece[:, 64:96]

    for copy in loads:
        copy.wait()
    start_halo(0, 0)
    for elem in (1, 2):
        split_main(0, 0, elem)

    all_turned = pltpu.make_async_remote_copy(
        src_ref=turned.at[pl.ds(0, passes - 1)], dst_ref=turned.at[pl.ds(0, passes - 1)],
        send_sem=turn_send, recv_sem=turn_recv, device_id=(row, up, span), device_id_type=MESH)
    all_turned.wait()
    total = LANES * passes
    shift = lax.rem(lax.rem(offset[0], total) + total, total)
    shift = jnp.where(row == 0, shift, lax.rem(total - shift, total))
    places = shift // LANES
    within = lax.rem(shift, LANES)
    tile_lane = lax.broadcasted_iota(jnp.int32, (tile, LANES), 1)

    def rotate(step, carry):
        other = peer(step)
        near = turned[lax.rem(other - places + passes, passes)]
        far = turned[lax.rem(other - places + 2 * passes - 1, passes)]
        ready[other] = pltpu.roll(jnp.where(tile_lane < LANES - within, near, far), within, 1)
        pltpu.make_async_remote_copy(
            src_ref=ready.at[other], dst_ref=facing.at[pl.ds(pl.multiple_of(tile * here, tile), tile)],
            send_sem=face_send, recv_sem=face_recv, device_id=(1 - row, other, span), device_id_type=MESH,
        ).start()
        return carry

    lax.fori_loop(0, passes, rotate, 0, unroll=4)

    wait_halo(0, 0)
    for elem in (0, 3):
        split_main(0, 0, elem)
    split_ghosts(0, 0)
    for copy in old_loads:
        copy.wait()

    def store_residual(j, mine, part):
        resid[j] = INV_DT * (mine - resid[j]) + part

    apply(0, 0, store_residual)

    all_faced = pltpu.make_async_remote_copy(
        src_ref=facing, dst_ref=facing, send_sem=face_send, recv_sem=face_recv,
        device_id=(1 - row, here, span), device_id_type=MESH)
    all_faced.wait()

    for j in range(SLICES):
        block = facing[pl.ds(j, 25, stride=SLICES), :]
        block = jnp.concatenate([block, jnp.zeros((7, LANES), jnp.float32)], axis=0)
        for half, piece in enumerate(halves(block)):
            face_x[j // 4, pl.ds(32 * half, 32), pl.ds(LANES * (j % 4), LANES)] = piece
    outs = [
        pltpu.make_async_copy(resid.at[j, pl.ds(0, 125)], residual_out.at[:, j, 0, :], out_sem.at[0, j])
        for j in range(SLICES)
    ]
    for s in range(5):
        image = jnp.dot(face_op[...], face_x[s], preferred_element_type=jnp.float32)
        image = image[0:SLICE] + image[SLICE : 2 * SLICE]
        for elem in range(4):
            j = 4 * s + elem
            whole = resid[j] + image[:, LANES * elem : LANES * (elem + 1)]
            resid[j] = whole
            values[1, pl.ds(SLICE * j, SLICE), :] = whole * (-1.0 / DIAG)
    for copy in outs:
        copy.start()

    rate = OMEGA / DIAG

    def sweep(t, carry):
        slot = lax.rem(t, 2)
        start_halo(slot, t)
        for elem in (1, 2):
            split_main(slot, t, elem)
        wait_halo(slot, t)
        for elem in (0, 3):
            split_main(slot, t, elem)
        split_ghosts(slot, t)

        def store(j, mine, part):
            image = (INV_DT + INV_DTAU) * mine + part
            values[1 - slot, pl.ds(SLICE * j, SLICE), :] = mine - rate * (resid[j] + image)

        apply(slot, t, store)
        return carry

    lax.fori_loop(1, SWEEPS + 1, sweep, 0)

    last = (SWEEPS + 1) % 2
    final = [
        pltpu.make_async_copy(
            values.at[last, pl.ds(SLICE * j, 125)], update_out.at[:, j, 0, :], out_sem.at[1, j]
        )
        for j in range(SLICES)
    ]
    for copy in final:
        copy.start()
    for copy in outs + final:
        copy.wait()


def per_device(passes, state, old_state, jacobians, offset):
    shape = state.shape
    tile = TRACE // passes
    anywhere = pl.BlockSpec(memory_space=pl.ANY)
    in_hbm = pl.BlockSpec(memory_space=pltpu.HBM)
    f32, bf16, dma = jnp.float32, jnp.bfloat16, pltpu.SemaphoreType.DMA
    exchanges = SWEEPS + 1
    viewed = (125, SLICES, 1, LANES)
    pinned = lambda x: pltpu.with_memory_space_constraint(x, pltpu.HBM)
    outs = pl.pallas_call(
        functools.partial(kernel, passes),
        out_shape=[jax.ShapeDtypeStruct(viewed, f32)] * 2,
        in_specs=[in_hbm, in_hbm, in_hbm,
                  pl.BlockSpec(memory_space=pltpu.SMEM), in_hbm],
        out_specs=[anywhere] * 2,
        scratch_shapes=[
            pltpu.VMEM((2, SLICE * SLICES + 40, LANES), f32),
            pltpu.VMEM((SLICES, SLICE, LANES), f32),
            pltpu.VMEM((26, SLICES, 1, LANES), f32),
            pltpu.VMEM((passes, tile, LANES), f32),
            pltpu.VMEM((passes, tile, LANES), f32),
            pltpu.VMEM((TRACE, LANES), f32),
            pltpu.VMEM((13, SLICE, SLICE), f32),
            pltpu.VMEM((3, 8, LANES), f32),
            pltpu.VMEM((5, 3, 5), f32),
            pltpu.VMEM((2 * SLICE, 4 * SLICE), bf16),
            pltpu.VMEM((2 * SLICE, 128), bf16),
            pltpu.VMEM((2 * SLICE, 64), bf16),
            pltpu.VMEM((5, 4 * SLICE, 4 * LANES), bf16),
            pltpu.VMEM((5, 128, 4 * LANES), bf16),
            pltpu.VMEM((5, 64, 4 * LANES), bf16),
            pltpu.VMEM((exchanges, 32, LANES), f32),
            pltpu.VMEM((exchanges, 32, LANES), f32),
            pltpu.VMEM((exchanges, 32, LANES), f32),
            pltpu.VMEM((exchanges, 32, LANES), f32),
            pltpu.VMEM((exchanges, SLICE, LANES), f32),
            dma((SLICES,)), dma((SLICES,)), dma((5,)), dma, dma, dma((2, SLICES)),
            dma, dma, dma, dma, dma((3, exchanges)), dma((3, exchanges)),
        ],
        compiler_params=pltpu.CompilerParams(
            collective_id=0, has_side_effects=True, vmem_limit_bytes=48 * 1024 * 1024
        ),
        name="pseudo_step",
    )(
        pinned(state.reshape(viewed)), pinned(old_state.reshape(viewed)),
        pinned(jnp.transpose(jacobians, (1, 0, 2))), offset, pinned(jnp.asarray(operator_patterns())),
    )
    return tuple(out.reshape(shape) for out in outs)


def solution(mesh):
    placed = P("row", None, None, None, "span", "pass")
    return jax.shard_map(
        functools.partial(per_device, mesh.shape["pass"]),
        mesh=mesh,
        in_specs=(placed, placed, P(), P()),
        out_specs=(placed, placed),
        check_vma=False,
    )
```

```python
import functools
import math

import jax
import jax.numpy as jnp
import numpy as np
from jax import lax
from jax.experimental import pallas as pl
from jax.experimental.pallas import tpu as pltpu
from jax.sharding import PartitionSpec as P

SWEEPS = 3
LIFT_HALF = 5.0
INV_DT = 1.5
INV_DTAU = 1.0
DIAG = 12.0
OMEGA = 0.7

LANES = 128
SLICE = 128
SLICES = 20
TRACE = 512
MESH = pl.DeviceIdType.MESH
HIGHEST = lax.Precision.HIGHEST


def gll_derivative():
    nodes = np.array([-1.0, -math.sqrt(3.0 / 7.0), 0.0, math.sqrt(3.0 / 7.0), 1.0])
    legend = (35.0 * nodes**4 - 30.0 * nodes**2 + 3.0) / 8.0
    table = np.zeros((5, 5))
    for left in range(5):
        for right in range(5):
            if left != right:
                table[left, right] = legend[left] / (legend[right] * (nodes[left] - nodes[right]))
    return table


def operator_patterns():
    deriv = gll_derivative()
    planes = np.zeros((13, SLICE, SLICE), np.float32)
    places = [(v, a, p) for v in range(5) for a in range(5) for p in range(5)]
    for q, (v, a, p) in enumerate(places):
        planes[12, q, v] = 1.0
        planes[4, v, q] = 1.0
        planes[3, q, q] = LIFT_HALF * ((a in (0, 4)) + (p in (0, 4)))
        for c, (w, b, r) in enumerate(places):
            planes[0, q, c] = deriv[a, b] * (p == r)
            planes[1, q, c] = deriv[p, r] * (a == b)
            planes[2, q, c] = (a == b) * (p == r)
        for w in range(5):
            for k in range(5):
                low, high, face = 5 * w + k, 32 + 5 * w + k, 64 + 5 * w + k
                if p == 0 and a == k:
                    planes[7, q, low] = -LIFT_HALF
                    planes[8:10, q, low] = -LIFT_HALF * (v == w)
                if p == 4 and a == k:
                    planes[7, q, high] = LIFT_HALF
                    planes[8:10, q, high] = -LIFT_HALF * (v == w)
                if a == 4 and p == k:
                    planes[10, q, face] = LIFT_HALF
                    planes[8, q, face] = -LIFT_HALF * (v == w)
                if a == 0 and p == k:
                    planes[11, q, face] = -LIFT_HALF
                    planes[9, q, face] = -LIFT_HALF * (v == w)
    for w in range(5):
        planes[5, w, 5 * w : 5 * w + 5] = 1.0
        planes[5, w, 32 + 5 * w : 32 + 5 * w + 5] = 1.0
        planes[6, w, 64 + 5 * w : 64 + 5 * w + 5] = 1.0
    return planes


def halves(x):
    high = x.astype(jnp.bfloat16)
    low = (x - high.astype(jnp.float32)).astype(jnp.bfloat16)
    return high, low


def kernel(
    passes,
    state, older, jacobians, offset, planes,
    resid_rows, update_rows,
    resid, even, odd, trace, turned, ready, facing, pats, spread, jacs, edge_rows,
    main_op, face_op, span_op, pitch_op, main_x, face_x,
    pack_up, pack_down, from_low, from_high, from_span,
    load_sem, old_sem, trace_sem, pat_sem, jac_sem,
    turn_send, turn_recv, face_send, face_recv, halo_send, halo_recv,
):
    values = (even, odd)
    row, here, span = lax.axis_index("row"), lax.axis_index("pass"), lax.axis_index("span")
    up, down = lax.rem(here + 1, passes), lax.rem(here + passes - 1, passes)
    tile = TRACE // passes
    deriv = gll_derivative()

    def peer(step):
        turn_z, turn_y, turn_core = step // 8, lax.rem(step // 2, 4), lax.rem(step + 1, 2)
        along_z = 4 + (1 - 2 * lax.rem(turn_z, 2)) * ((turn_z + 1) // 2)
        along_y = 2 + (1 - 2 * lax.rem(turn_y, 2)) * ((turn_y + 1) // 2)
        y = lax.rem(here // 16 + along_y, 4)
        z = lax.rem(here // 2 + along_z, 8)
        return 16 * y + 2 * z + lax.rem(here + turn_core, 2)

    barrier = pltpu.get_barrier_semaphore()

    def greet(step, carry):
        other = peer(step)
        pl.semaphore_signal(barrier, inc=1, device_id=(1 - row, other, span), device_id_type=MESH)
        pl.semaphore_signal(barrier, inc=1, device_id=(row, other, span), device_id_type=MESH)
        return carry

    lax.fori_loop(0, passes - 1, greet, 0)
    pl.semaphore_signal(barrier, inc=1, device_id=(1 - row, here, span), device_id_type=MESH)
    pl.semaphore_signal(barrier, inc=1, device_id=(row, here, 1 - span), device_id_type=MESH)

    loads = [
        pltpu.make_async_copy(state.at[:, j, 0, :], even.at[pl.ds(SLICE * j, 125)], load_sem.at[j])
        for j in range(SLICES)
    ]
    old_loads = [
        pltpu.make_async_copy(older.at[:, j, 0, :], resid.at[pl.ds(SLICE * j, 125)], old_sem.at[j])
        for j in range(SLICES)
    ]
    plane_at = 20 * (1 - row)
    trace_loads = [
        pltpu.make_async_copy(
            state.at[pl.ds(25 * v + plane_at, 5)], trace.at[pl.ds(5 * v, 5)], trace_sem.at[v]
        )
        for v in range(5)
    ]
    pat_load = pltpu.make_async_copy(planes, pats, pat_sem)
    jac_load = pltpu.make_async_copy(jacobians, jacs, jac_sem)
    for copy in trace_loads + loads + [pat_load, jac_load] + old_loads:
        copy.start()

    lane = lax.broadcasted_iota(jnp.int32, (32, LANES), 1)
    sent = (SLICES - 1) * (1 - span)
    sent_rows = pl.ds(pl.multiple_of(SLICE * sent, SLICE), SLICE)

    def pitch_rows(field, j, node):
        return field[pl.ds(SLICE * j + node, 32, stride=5), :]

    def span_copy(field, t):
        return pltpu.make_async_remote_copy(
            src_ref=field.at[sent_rows], dst_ref=from_span.at[t],
            send_sem=halo_send.at[0, t], recv_sem=halo_recv.at[0, t],
            device_id=(row, here, 1 - span), device_id_type=MESH)

    def pitch_copies(t):
        return [
            pltpu.make_async_remote_copy(
                src_ref=pack_up.at[t], dst_ref=from_low.at[t],
                send_sem=halo_send.at[1, t], recv_sem=halo_recv.at[1, t],
                device_id=(row, up, span), device_id_type=MESH),
            pltpu.make_async_remote_copy(
                src_ref=pack_down.at[t], dst_ref=from_high.at[t],
                send_sem=halo_send.at[2, t], recv_sem=halo_recv.at[2, t],
                device_id=(row, down, span), device_id_type=MESH),
        ]

    def packed(field):
        upward = jnp.zeros((32, LANES), jnp.float32)
        downward = jnp.zeros((32, LANES), jnp.float32)
        for j in range(SLICES):
            upward = jnp.where(lane == j, pltpu.roll(pitch_rows(field, j, 4), j + 1, 1), upward)
            first = pitch_rows(field, j, 0)
            downward = jnp.where(lane == j, pltpu.roll(first, j, 1) if j else first, downward)
        return upward, downward

    def split_main(field, elem):
        cols = pl.ds(LANES * elem, LANES)

        def chunk(c, carry):
            at = pl.multiple_of(16 * c, 16)
            load = lambda j: field[pl.ds(pl.multiple_of(SLICE * j + at, 16), 16), :]
            v = [load(4 * s + elem) for s in range(5)]
            sum04, dif04, sum13, dif13 = v[0] + v[4], v[0] - v[4], v[1] + v[3], v[1] - v[3]
            d = lambda i, j: float(deriv[i, j])
            odd0 = (0.5 * (d(0, 1) + d(0, 3))) * sum13 + d(0, 2) * v[2] + (0.5 * d(0, 4)) * sum04
            even0 = (0.5 * (d(0, 1) - d(0, 3))) * dif13 - (0.5 * d(0, 4)) * dif04
            odd1 = (0.5 * (d(1, 0) + d(1, 4))) * sum04 + d(1, 2) * v[2] + (0.5 * d(1, 3)) * sum13
            even1 = (0.5 * (d(1, 0) - d(1, 4))) * dif04 - (0.5 * d(1, 3)) * dif13
            g = [
                even0 + odd0,
                even1 + odd1,
                d(2, 0) * dif04 + d(2, 1) * dif13,
                even1 - odd1,
                even0 - odd0,
            ]
            if elem > 0:
                g[0] = g[0] - LIFT_HALF * load(16 + elem - 1)
            if elem < 3:
                g[4] = g[4] + LIFT_HALF * load(elem + 1)
            for s in range(5):
                for part, block in enumerate((v[s], g[s])):
                    for half, piece in enumerate(halves(block)):
                        place = 2 * SLICE * half + SLICE * part
                        main_x[s, pl.ds(pl.multiple_of(place + at, 16), 16), cols] = piece
            return carry

        lax.fori_loop(0, SLICE // 16, chunk, 0)

    def split_ghosts(field):
        for j in range(SLICES):
            cols = pl.ds(LANES * (j % 4), LANES)
            low = jnp.where(lane == 0, 0.0, pltpu.roll(pitch_rows(field, j, 4), 1, 1))
            high = jnp.where(lane == LANES - 1, 0.0, pltpu.roll(pitch_rows(field, j, 0), LANES - 1, 1))
            for part, block in enumerate((low, high)):
                for half, piece in enumerate(halves(block)):
                    main_x[j // 4, pl.ds(4 * SLICE + 64 * half + 32 * part, 32), cols] = piece

    def apply(field, store):
        for elem in range(4):
            split_main(field, elem)
        split_ghosts(field)
        for s in range(5):
            image = jnp.dot(main_op[...], main_x[s], preferred_element_type=jnp.float32)
            image = image[0:SLICE] + image[SLICE : 2 * SLICE]
            for elem in range(4):
                j = 4 * s + elem
                mine = field[pl.ds(SLICE * j, SLICE), :]
                part = image[:, LANES * elem : LANES * (elem + 1)]
                if s in (0, 4):
                    jump = mine
                    if s == 0 and elem > 0:
                        jump = mine - field[pl.ds(SLICE * (16 + elem - 1), SLICE), :]
                    if s == 4 and elem < 3:
                        jump = mine - field[pl.ds(SLICE * (elem + 1), SLICE), :]
                    part = part + LIFT_HALF * jump
                store(j, mine, part)

    def correct(field, t, factor, send_on):
        if send_on:
            upward, downward = packed(field)
        for copy in pitch_copies(t):
            copy.wait()
        pieces = [piece for got in (from_low[t], from_high[t]) for piece in halves(got)]
        edge = jnp.dot(pitch_op[...], jnp.concatenate(pieces, 0), preferred_element_type=jnp.float32)
        low = factor * (edge[0:32] + edge[32:64])
        high = factor * (edge[64:96] + edge[96:128])
        span_copy(field, t).wait()
        share = jnp.dot(span_op[...], jnp.concatenate(halves(from_span[t]), 0), preferred_element_type=jnp.float32)
        field[sent_rows, :] = field[sent_rows, :] + factor * (share[0:SLICE] + share[SLICE : 2 * SLICE])

        def columns(j):
            at_low = pl.ds(SLICE * j, 25, stride=5)
            at_high = pl.ds(SLICE * j + 4, 25, stride=5)
            came = pltpu.roll(low, lax.rem(LANES - j, LANES), 1)
            field[at_low, :] = field[at_low, :] + jnp.where(lane == 0, came, 0.0)[0:25]
            came = pltpu.roll(high, LANES - 1 - j, 1)
            field[at_high, :] = field[at_high, :] + jnp.where(lane == LANES - 1, came, 0.0)[0:25]

        columns(sent)
        if send_on:
            span_copy(field, t + 1).start()
            last = pltpu.roll(pitch_rows(field, sent, 4), sent + 1, 1)
            first = pltpu.roll(pitch_rows(field, sent, 0), sent, 1)
            pack_up[t + 1] = jnp.where(lane == sent, last, upward + high)
            pack_down[t + 1] = jnp.where(lane == sent, first, downward + low)
            for copy in pitch_copies(t + 1):
                copy.start()
        columns(SLICES - 1 - sent)
        for j in range(1, SLICES - 1):
            columns(j)

    trace[pl.ds(25, 1)] = jnp.zeros((1, SLICES, 1, LANES), jnp.float32)
    for copy in trace_loads:
        copy.wait()
    pl.semaphore_wait(barrier, 2 * passes)
    flat = trace.reshape(26 * SLICES, LANES)

    def turn_copy(other):
        return pltpu.make_async_remote_copy(
            src_ref=flat.at[pl.ds(pl.multiple_of(tile * other, tile), tile)], dst_ref=turned.at[here],
            send_sem=turn_send, recv_sem=turn_recv, device_id=(row, other, span), device_id_type=MESH)

    def turn(step, carry):
        turn_copy(peer(step)).start()
        return carry

    lax.fori_loop(0, passes - 1, turn, 0)
    turned[here] = flat[pl.ds(pl.multiple_of(tile * here, tile), tile), :]

    for field in (even, resid):
        for j in range(SLICES):
            field[pl.ds(SLICE * j + 125, 3), :] = jnp.zeros((3, LANES), jnp.float32)
    for field in (even, odd):
        field[pl.ds(SLICE * SLICES, 40), :] = jnp.zeros((40, LANES), jnp.float32)

    pat_load.wait()
    jac_load.wait()
    spread[...] = jnp.zeros_like(spread)
    for d in range(3):
        spread[d, 0:5, 0:5] = jacs[:, d, :]
    rows = pats[12][:, 0:8]

    def spread_out(d, plane):
        by_row = jnp.dot(rows, spread[d], precision=HIGHEST, preferred_element_type=jnp.float32)
        return jnp.dot(by_row, pats[plane], precision=HIGHEST, preferred_element_type=jnp.float32)

    own = spread_out(0, 4) * pats[0] + spread_out(1, 4) * pats[1] + pats[3]
    along = spread_out(2, 4) * pats[2]
    edges = spread_out(1, 5) * pats[7] + spread_out(0, 6) * pats[10 + row] + pats[8 + row]
    for half in range(2):
        op_rows = pl.ds(SLICE * half, SLICE)
        for part, block in enumerate((own, along)):
            piece = halves(block)[half]
            for again in range(2):
                main_op[op_rows, pl.ds(2 * SLICE * again + SLICE * part, SLICE)] = piece
        piece = halves(edges)[half]
        for again in range(2):
            main_op[op_rows, pl.ds(4 * SLICE + 64 * again, 64)] = piece[:, 0:64]
            face_op[op_rows, pl.ds(32 * again, 32)] = piece[:, 64:96]
    square = (SLICE, SLICE)
    same = lax.broadcasted_iota(jnp.int32, square, 0) == lax.broadcasted_iota(jnp.int32, square, 1)
    outer = jnp.where(span == 0, LIFT_HALF, -LIFT_HALF) * along - jnp.where(same, LIFT_HALF, 0.0)
    edge_rows[pl.ds(0, SLICE), :] = edges
    edge_rows[pl.ds(SLICE, 32), :] = jnp.zeros((32, LANES), jnp.float32)
    lows = edge_rows[pl.ds(0, 32, stride=5), :][:, 0:32]
    highs = edge_rows[pl.ds(4, 32, stride=5), :][:, 32:64]
    pitch_op[...] = jnp.zeros_like(pitch_op)
    for half in range(2):
        for again in range(2):
            span_op[pl.ds(SLICE * half, SLICE), pl.ds(SLICE * again, SLICE)] = halves(outer)[half]
            pitch_op[pl.ds(32 * half, 32), pl.ds(32 * again, 32)] = halves(lows)[half]
            pitch_op[pl.ds(64 + 32 * half, 32), pl.ds(64 + 32 * again, 32)] = halves(highs)[half]

    for copy in loads:
        copy.wait()
    span_copy(even, 0).start()
    pack_up[0], pack_down[0] = packed(even)
    for copy in pitch_copies(0):
        copy.start()

    all_turned = pltpu.make_async_remote_copy(
        src_ref=turned.at[pl.ds(0, passes - 1)], dst_ref=turned.at[pl.ds(0, passes - 1)],
        send_sem=turn_send, recv_sem=turn_recv, device_id=(row, up, span), device_id_type=MESH)
    all_turned.wait()
    total = LANES * passes
    shift = lax.rem(lax.rem(offset[0], total) + total, total)
    shift = jnp.where(row == 0, shift, lax.rem(total - shift, total))
    places = shift // LANES
    within = lax.rem(shift, LANES)
    tile_lane = lax.broadcasted_iota(jnp.int32, (tile, LANES), 1)

    def rotate(step, carry):
        other = peer(step)
        near = turned[lax.rem(other - places + passes, passes)]
        far = turned[lax.rem(other - places + 2 * passes - 1, passes)]
        ready[other] = pltpu.roll(jnp.where(tile_lane < LANES - within, near, far), within, 1)
        pltpu.make_async_remote_copy(
            src_ref=ready.at[other], dst_ref=facing.at[pl.ds(pl.multiple_of(tile * here, tile), tile)],
            send_sem=face_send, recv_sem=face_recv, device_id=(1 - row, other, span), device_id_type=MESH,
        ).start()
        return carry

    lax.fori_loop(0, passes, rotate, 0, unroll=4)

    for copy in old_loads:
        copy.wait()

    def store_residual(j, mine, part):
        at = pl.ds(SLICE * j, SLICE)
        resid[at, :] = INV_DT * (mine - resid[at, :]) + part

    apply(even, store_residual)
    correct(resid, 0, 1.0, False)

    all_faced = pltpu.make_async_remote_copy(
        src_ref=facing, dst_ref=facing, send_sem=face_send, recv_sem=face_recv,
        device_id=(1 - row, here, span), device_id_type=MESH)
    all_faced.wait()

    for j in range(SLICES):
        block = facing[pl.ds(j, 25, stride=SLICES), :]
        block = jnp.concatenate([block, jnp.zeros((7, LANES), jnp.float32)], axis=0)
        for half, piece in enumerate(halves(block)):
            face_x[j // 4, pl.ds(32 * half, 32), pl.ds(LANES * (j % 4), LANES)] = piece
    for s in (0, 4, 1, 2, 3):
        image = jnp.dot(face_op[...], face_x[s], preferred_element_type=jnp.float32)
        image = image[0:SLICE] + image[SLICE : 2 * SLICE]
        for elem in range(4):
            at = pl.ds(SLICE * (4 * s + elem), SLICE)
            whole = resid[at, :] + image[:, LANES * elem : LANES * (elem + 1)]
            resid[at, :] = whole
            odd[at, :] = whole * (-1.0 / DIAG)
        if s == 4:
            span_copy(odd, 1).start()
    pack_up[1], pack_down[1] = packed(odd)
    for copy in pitch_copies(1):
        copy.start()

    def interleave(field, rows):
        flat_rows = rows.reshape(125 * SLICES, LANES)
        for j in range(SLICES):
            flat_rows[pl.ds(j, 125, stride=SLICES), :] = field[pl.ds(SLICE * j, 125), :]

    interleave(resid, resid_rows)
    rate = OMEGA / DIAG
    for t in range(1, SWEEPS + 1):
        field, after = values[t % 2], values[1 - t % 2]

        def store(j, mine, part):
            at = pl.ds(SLICE * j, SLICE)
            image = (INV_DT + INV_DTAU) * mine + part
            after[at, :] = mine - rate * (resid[at, :] + image)

        apply(field, store)
        correct(after, t, -rate, t < SWEEPS)
    interleave(values[(SWEEPS + 1) % 2], update_rows)


def write_kernel(resid, update, residual_out, update_out, sems):
    copies = [
        pltpu.make_async_copy(rows, out, sems.at[k])
        for k, (rows, out) in enumerate(((update, update_out), (resid, residual_out)))
    ]
    for copy in copies:
        copy.start()
    for copy in copies:
        copy.wait()


def per_device(passes, state, old_state, jacobians, offset):
    shape = state.shape
    tile = TRACE // passes
    in_hbm = pl.BlockSpec(memory_space=pltpu.HBM)
    f32, bf16, dma = jnp.float32, jnp.bfloat16, pltpu.SemaphoreType.DMA
    exchanges = SWEEPS + 1
    viewed = (125, SLICES, 1, LANES)
    pinned = lambda x: pltpu.with_memory_space_constraint(x, pltpu.HBM)
    in_vmem = pl.BlockSpec(memory_space=pltpu.VMEM)
    slices = (SLICE * SLICES + 40, LANES)
    fields = pl.pallas_call(
        functools.partial(kernel, passes),
        out_shape=[jax.ShapeDtypeStruct((625, 4, LANES), f32)] * 2,
        in_specs=[in_hbm, in_hbm, in_hbm, pl.BlockSpec(memory_space=pltpu.SMEM), in_hbm],
        out_specs=[in_vmem] * 2,
        scratch_shapes=[
            pltpu.VMEM(slices, f32),
            pltpu.VMEM(slices, f32),
            pltpu.VMEM(slices, f32),
            pltpu.VMEM((26, SLICES, 1, LANES), f32),
            pltpu.VMEM((passes, tile, LANES), f32),
            pltpu.VMEM((passes, tile, LANES), f32),
            pltpu.VMEM((TRACE, LANES), f32),
            pltpu.VMEM((13, SLICE, SLICE), f32),
            pltpu.VMEM((3, 8, LANES), f32),
            pltpu.VMEM((5, 3, 5), f32),
            pltpu.VMEM((SLICE + 32, LANES), f32),
            pltpu.VMEM((2 * SLICE, 5 * SLICE), bf16),
            pltpu.VMEM((2 * SLICE, 64), bf16),
            pltpu.VMEM((2 * SLICE, 2 * SLICE), bf16),
            pltpu.VMEM((128, 128), bf16),
            pltpu.VMEM((5, 5 * SLICE, 4 * LANES), bf16),
            pltpu.VMEM((5, 64, 4 * LANES), bf16),
            pltpu.VMEM((exchanges, 32, LANES), f32),
            pltpu.VMEM((exchanges, 32, LANES), f32),
            pltpu.VMEM((exchanges, 32, LANES), f32),
            pltpu.VMEM((exchanges, 32, LANES), f32),
            pltpu.VMEM((exchanges, SLICE, LANES), f32),
            dma((SLICES,)), dma((SLICES,)), dma((5,)), dma, dma,
            dma, dma, dma, dma, dma((3, exchanges)), dma((3, exchanges)),
        ],
        compiler_params=pltpu.CompilerParams(
            collective_id=0, has_side_effects=True, vmem_limit_bytes=40 * 1024 * 1024
        ),
        name="pseudo_step",
    )(
        pinned(state.reshape(viewed)), pinned(old_state.reshape(viewed)),
        pinned(jnp.transpose(jacobians, (1, 0, 2))), offset, pinned(jnp.asarray(operator_patterns())),
    )
    outs = pl.pallas_call(
        write_kernel,
        out_shape=[jax.ShapeDtypeStruct((625, 4, LANES), f32)] * 2,
        in_specs=[pl.BlockSpec(memory_space=pl.ANY)] * 2,
        out_specs=[in_hbm] * 2,
        scratch_shapes=[dma((2,))],
        compiler_params=pltpu.CompilerParams(vmem_limit_bytes=1024 * 1024),
        name="write_fields",
    )(*fields)
    return tuple(out.reshape(shape) for out in outs)


def solution(mesh):
    placed = P("row", None, None, None, "span", "pass")
    return jax.shard_map(
        functools.partial(per_device, mesh.shape["pass"]),
        mesh=mesh,
        in_specs=(placed, placed, P(), P()),
        out_specs=(placed, placed),
        check_vma=False,
    )
```

```python
import functools
import math

import jax
import jax.numpy as jnp
import numpy as np
from jax import lax
from jax.experimental import pallas as pl
from jax.experimental.pallas import tpu as pltpu
from jax.sharding import PartitionSpec as P

SWEEPS = 3
LIFT_HALF = 5.0
INV_DT = 1.5
INV_DTAU = 1.0
DIAG = 12.0
OMEGA = 0.7

LANES = 128
SLICE = 128
SLICES = 20
TRACE = 512
MESH = pl.DeviceIdType.MESH
HIGHEST = lax.Precision.HIGHEST


def gll_derivative():
    nodes = np.array([-1.0, -math.sqrt(3.0 / 7.0), 0.0, math.sqrt(3.0 / 7.0), 1.0])
    legend = (35.0 * nodes**4 - 30.0 * nodes**2 + 3.0) / 8.0
    table = np.zeros((5, 5))
    for left in range(5):
        for right in range(5):
            if left != right:
                table[left, right] = legend[left] / (legend[right] * (nodes[left] - nodes[right]))
    return table


def operator_patterns():
    deriv = gll_derivative()
    planes = np.zeros((13, SLICE, SLICE), np.float32)
    places = [(v, a, p) for v in range(5) for a in range(5) for p in range(5)]
    for q, (v, a, p) in enumerate(places):
        planes[12, q, v] = 1.0
        planes[4, v, q] = 1.0
        planes[3, q, q] = LIFT_HALF * ((a in (0, 4)) + (p in (0, 4)))
        for c, (w, b, r) in enumerate(places):
            planes[0, q, c] = deriv[a, b] * (p == r)
            planes[1, q, c] = deriv[p, r] * (a == b)
            planes[2, q, c] = (a == b) * (p == r)
        for w in range(5):
            for k in range(5):
                low, high, face = 5 * w + k, 32 + 5 * w + k, 64 + 5 * w + k
                if p == 0 and a == k:
                    planes[7, q, low] = -LIFT_HALF
                    planes[8:10, q, low] = -LIFT_HALF * (v == w)
                if p == 4 and a == k:
                    planes[7, q, high] = LIFT_HALF
                    planes[8:10, q, high] = -LIFT_HALF * (v == w)
                if a == 4 and p == k:
                    planes[10, q, face] = LIFT_HALF
                    planes[8, q, face] = -LIFT_HALF * (v == w)
                if a == 0 and p == k:
                    planes[11, q, face] = -LIFT_HALF
                    planes[9, q, face] = -LIFT_HALF * (v == w)
    for w in range(5):
        planes[5, w, 5 * w : 5 * w + 5] = 1.0
        planes[5, w, 32 + 5 * w : 32 + 5 * w + 5] = 1.0
        planes[6, w, 64 + 5 * w : 64 + 5 * w + 5] = 1.0
    return planes


def halves(x):
    high = x.astype(jnp.bfloat16)
    low = (x - high.astype(jnp.float32)).astype(jnp.bfloat16)
    return high, low


def kernel(
    passes,
    state, older, jacobians, offset, planes,
    resid_rows, update_rows,
    resid, even, odd, trace, turned, ready, facing, pats, spread, jacs, edge_rows,
    main_op, face_op, span_op, pitch_op, main_x, face_x,
    pack_up, pack_down, from_low, from_high, from_span,
    load_sem, old_sem, trace_sem, pat_sem, jac_sem,
    row_sem, turn_send, turn_recv, face_send, face_recv, halo_send, halo_recv,
):
    values = (even, odd)
    row, here, span = lax.axis_index("row"), lax.axis_index("pass"), lax.axis_index("span")
    up, down = lax.rem(here + 1, passes), lax.rem(here + passes - 1, passes)
    tile = TRACE // passes
    deriv = gll_derivative()

    def peer(step):
        turn_z, turn_y, turn_core = step // 8, lax.rem(step // 2, 4), lax.rem(step + 1, 2)
        along_z = 4 + (1 - 2 * lax.rem(turn_z, 2)) * ((turn_z + 1) // 2)
        along_y = 2 + (1 - 2 * lax.rem(turn_y, 2)) * ((turn_y + 1) // 2)
        y = lax.rem(here // 16 + along_y, 4)
        z = lax.rem(here // 2 + along_z, 8)
        return 16 * y + 2 * z + lax.rem(here + turn_core, 2)

    barrier = pltpu.get_barrier_semaphore()

    def greet(step, carry):
        other = peer(step)
        pl.semaphore_signal(barrier, inc=1, device_id=(row, other, span), device_id_type=MESH)
        return carry

    lax.fori_loop(0, passes - 1, greet, 0)
    pl.semaphore_signal(barrier, inc=1, device_id=(1 - row, here, span), device_id_type=MESH)
    pl.semaphore_signal(barrier, inc=1, device_id=(row, here, 1 - span), device_id_type=MESH)

    loads = [
        pltpu.make_async_copy(state.at[:, j, 0, :], even.at[pl.ds(SLICE * j, 125)], load_sem.at[j])
        for j in range(SLICES)
    ]
    old_loads = [
        pltpu.make_async_copy(older.at[:, j, 0, :], resid.at[pl.ds(SLICE * j, 125)], old_sem.at[j])
        for j in range(SLICES)
    ]
    plane_at = 20 * (1 - row)
    trace_loads = [
        pltpu.make_async_copy(
            state.at[pl.ds(25 * v + plane_at, 5)], trace.at[pl.ds(5 * v, 5)], trace_sem.at[v]
        )
        for v in range(5)
    ]
    pat_load = pltpu.make_async_copy(planes, pats, pat_sem)
    jac_load = pltpu.make_async_copy(jacobians, jacs, jac_sem)
    for copy in trace_loads + loads + [pat_load, jac_load] + old_loads:
        copy.start()

    lane = lax.broadcasted_iota(jnp.int32, (32, LANES), 1)
    sent = (SLICES - 1) * (1 - span)
    sent_rows = pl.ds(pl.multiple_of(SLICE * sent, SLICE), SLICE)

    def pitch_rows(field, j, node):
        return field[pl.ds(SLICE * j + node, 32, stride=5), :]

    def span_copy(field, t):
        return pltpu.make_async_remote_copy(
            src_ref=field.at[sent_rows], dst_ref=from_span.at[t],
            send_sem=halo_send.at[0, t], recv_sem=halo_recv.at[0, t],
            device_id=(row, here, 1 - span), device_id_type=MESH)

    def pitch_copies(t):
        return [
            pltpu.make_async_remote_copy(
                src_ref=pack_up.at[t], dst_ref=from_low.at[t],
                send_sem=halo_send.at[1, t], recv_sem=halo_recv.at[1, t],
                device_id=(row, up, span), device_id_type=MESH),
            pltpu.make_async_remote_copy(
                src_ref=pack_down.at[t], dst_ref=from_high.at[t],
                send_sem=halo_send.at[2, t], recv_sem=halo_recv.at[2, t],
                device_id=(row, down, span), device_id_type=MESH),
        ]

    def packed(field):
        upward = jnp.zeros((32, LANES), jnp.float32)
        downward = jnp.zeros((32, LANES), jnp.float32)
        for j in range(SLICES):
            upward = jnp.where(lane == j, pltpu.roll(pitch_rows(field, j, 4), j + 1, 1), upward)
            first = pitch_rows(field, j, 0)
            downward = jnp.where(lane == j, pltpu.roll(first, j, 1) if j else first, downward)
        return upward, downward

    def split_main(field, elem):
        cols = pl.ds(LANES * elem, LANES)

        def chunk(c, carry):
            at = pl.multiple_of(16 * c, 16)
            load = lambda j: field[pl.ds(pl.multiple_of(SLICE * j + at, 16), 16), :]
            v = [load(4 * s + elem) for s in range(5)]
            sum04, dif04, sum13, dif13 = v[0] + v[4], v[0] - v[4], v[1] + v[3], v[1] - v[3]
            d = lambda i, j: float(deriv[i, j])
            odd0 = (0.5 * (d(0, 1) + d(0, 3))) * sum13 + d(0, 2) * v[2] + (0.5 * d(0, 4)) * sum04
            even0 = (0.5 * (d(0, 1) - d(0, 3))) * dif13 - (0.5 * d(0, 4)) * dif04
            odd1 = (0.5 * (d(1, 0) + d(1, 4))) * sum04 + d(1, 2) * v[2] + (0.5 * d(1, 3)) * sum13
            even1 = (0.5 * (d(1, 0) - d(1, 4))) * dif04 - (0.5 * d(1, 3)) * dif13
            g = [
                even0 + odd0,
                even1 + odd1,
                d(2, 0) * dif04 + d(2, 1) * dif13,
                even1 - odd1,
                even0 - odd0,
            ]
            if elem > 0:
                g[0] = g[0] - LIFT_HALF * load(16 + elem - 1)
            if elem < 3:
                g[4] = g[4] + LIFT_HALF * load(elem + 1)
            for s in range(5):
                for part, block in enumerate((v[s], g[s])):
                    for half, piece in enumerate(halves(block)):
                        place = 2 * SLICE * half + SLICE * part
                        main_x[s, pl.ds(pl.multiple_of(place + at, 16), 16), cols] = piece
            return carry

        lax.fori_loop(0, SLICE // 16, chunk, 0)

    def split_ghosts(field):
        for j in range(SLICES):
            cols = pl.ds(LANES * (j % 4), LANES)
            low = jnp.where(lane == 0, 0.0, pltpu.roll(pitch_rows(field, j, 4), 1, 1))
            high = jnp.where(lane == LANES - 1, 0.0, pltpu.roll(pitch_rows(field, j, 0), LANES - 1, 1))
            for part, block in enumerate((low, high)):
                for half, piece in enumerate(halves(block)):
                    main_x[j // 4, pl.ds(4 * SLICE + 64 * half + 32 * part, 32), cols] = piece

    def apply(field, store):
        for elem in range(4):
            split_main(field, elem)
        split_ghosts(field)
        for s in range(5):
            image = jnp.dot(main_op[...], main_x[s], preferred_element_type=jnp.float32)
            image = image[0:SLICE] + image[SLICE : 2 * SLICE]
            for elem in range(4):
                j = 4 * s + elem
                mine = field[pl.ds(SLICE * j, SLICE), :]
                part = image[:, LANES * elem : LANES * (elem + 1)]
                if s in (0, 4):
                    jump = mine
                    if s == 0 and elem > 0:
                        jump = mine - field[pl.ds(SLICE * (16 + elem - 1), SLICE), :]
                    if s == 4 and elem < 3:
                        jump = mine - field[pl.ds(SLICE * (elem + 1), SLICE), :]
                    part = part + LIFT_HALF * jump
                store(j, mine, part)

    def correct(field, t, factor, send_on):
        if send_on:
            upward, downward = packed(field)
        for copy in pitch_copies(t):
            copy.wait()
        pieces = [piece for got in (from_low[t], from_high[t]) for piece in halves(got)]
        edge = jnp.dot(pitch_op[...], jnp.concatenate(pieces, 0), preferred_element_type=jnp.float32)
        low = factor * (edge[0:32] + edge[32:64])
        high = factor * (edge[64:96] + edge[96:128])
        span_copy(field, t).wait()
        share = jnp.dot(span_op[...], jnp.concatenate(halves(from_span[t]), 0), preferred_element_type=jnp.float32)
        field[sent_rows, :] = field[sent_rows, :] + factor * (share[0:SLICE] + share[SLICE : 2 * SLICE])

        def columns(j):
            at_low = pl.ds(SLICE * j, 25, stride=5)
            at_high = pl.ds(SLICE * j + 4, 25, stride=5)
            came = pltpu.roll(low, lax.rem(LANES - j, LANES), 1)
            field[at_low, :] = field[at_low, :] + jnp.where(lane == 0, came, 0.0)[0:25]
            came = pltpu.roll(high, LANES - 1 - j, 1)
            field[at_high, :] = field[at_high, :] + jnp.where(lane == LANES - 1, came, 0.0)[0:25]

        columns(sent)
        if send_on:
            span_copy(field, t + 1).start()
            last = pltpu.roll(pitch_rows(field, sent, 4), sent + 1, 1)
            first = pltpu.roll(pitch_rows(field, sent, 0), sent, 1)
            pack_up[t + 1] = jnp.where(lane == sent, last, upward + high)
            pack_down[t + 1] = jnp.where(lane == sent, first, downward + low)
            for copy in pitch_copies(t + 1):
                copy.start()
        columns(SLICES - 1 - sent)
        for j in range(1, SLICES - 1):
            columns(j)

    trace[pl.ds(25, 1)] = jnp.zeros((1, SLICES, 1, LANES), jnp.float32)
    for copy in trace_loads:
        copy.wait()
    pl.semaphore_wait(barrier, passes + 1)
    pl.semaphore_signal(row_sem, inc=1, device_id=(1 - row, here, span), device_id_type=MESH)
    flat = trace.reshape(26 * SLICES, LANES)

    def turn_copy(other):
        return pltpu.make_async_remote_copy(
            src_ref=flat.at[pl.ds(pl.multiple_of(tile * other, tile), tile)], dst_ref=turned.at[here],
            send_sem=turn_send, recv_sem=turn_recv, device_id=(row, other, span), device_id_type=MESH)

    def turn(step, carry):
        turn_copy(peer(step)).start()
        return carry

    lax.fori_loop(0, passes - 1, turn, 0)
    turned[here] = flat[pl.ds(pl.multiple_of(tile * here, tile), tile), :]

    for field in (even, resid):
        for j in range(SLICES):
            field[pl.ds(SLICE * j + 125, 3), :] = jnp.zeros((3, LANES), jnp.float32)
    for field in (even, odd):
        field[pl.ds(SLICE * SLICES, 40), :] = jnp.zeros((40, LANES), jnp.float32)

    pat_load.wait()
    jac_load.wait()
    spread[...] = jnp.zeros_like(spread)
    for d in range(3):
        spread[d, 0:5, 0:5] = jacs[:, d, :]
    rows = pats[12][:, 0:8]

    def spread_out(d, plane):
        by_row = jnp.dot(rows, spread[d], precision=HIGHEST, preferred_element_type=jnp.float32)
        return jnp.dot(by_row, pats[plane], precision=HIGHEST, preferred_element_type=jnp.float32)

    own = spread_out(0, 4) * pats[0] + spread_out(1, 4) * pats[1] + pats[3]
    along = spread_out(2, 4) * pats[2]
    edges = spread_out(1, 5) * pats[7] + spread_out(0, 6) * pats[10 + row] + pats[8 + row]
    for half in range(2):
        op_rows = pl.ds(SLICE * half, SLICE)
        for part, block in enumerate((own, along)):
            piece = halves(block)[half]
            for again in range(2):
                main_op[op_rows, pl.ds(2 * SLICE * again + SLICE * part, SLICE)] = piece
        piece = halves(edges)[half]
        for again in range(2):
            main_op[op_rows, pl.ds(4 * SLICE + 64 * again, 64)] = piece[:, 0:64]
            face_op[op_rows, pl.ds(32 * again, 32)] = piece[:, 64:96]
    square = (SLICE, SLICE)
    same = lax.broadcasted_iota(jnp.int32, square, 0) == lax.broadcasted_iota(jnp.int32, square, 1)
    outer = jnp.where(span == 0, LIFT_HALF, -LIFT_HALF) * along - jnp.where(same, LIFT_HALF, 0.0)
    edge_rows[pl.ds(0, SLICE), :] = edges
    edge_rows[pl.ds(SLICE, 32), :] = jnp.zeros((32, LANES), jnp.float32)
    lows = edge_rows[pl.ds(0, 32, stride=5), :][:, 0:32]
    highs = edge_rows[pl.ds(4, 32, stride=5), :][:, 32:64]
    pitch_op[...] = jnp.zeros_like(pitch_op)
    for half in range(2):
        for again in range(2):
            span_op[pl.ds(SLICE * half, SLICE), pl.ds(SLICE * again, SLICE)] = halves(outer)[half]
            pitch_op[pl.ds(32 * half, 32), pl.ds(32 * again, 32)] = halves(lows)[half]
            pitch_op[pl.ds(64 + 32 * half, 32), pl.ds(64 + 32 * again, 32)] = halves(highs)[half]

    for copy in loads:
        copy.wait()
    span_copy(even, 0).start()
    pack_up[0], pack_down[0] = packed(even)
    for copy in pitch_copies(0):
        copy.start()

    all_turned = pltpu.make_async_remote_copy(
        src_ref=turned.at[pl.ds(0, passes - 1)], dst_ref=turned.at[pl.ds(0, passes - 1)],
        send_sem=turn_send, recv_sem=turn_recv, device_id=(row, up, span), device_id_type=MESH)
    all_turned.wait()
    total = LANES * passes
    shift = lax.rem(lax.rem(offset[0], total) + total, total)
    shift = jnp.where(row == 0, shift, lax.rem(total - shift, total))
    places = shift // LANES
    within = lax.rem(shift, LANES)
    tile_lane = lax.broadcasted_iota(jnp.int32, (tile, LANES), 1)

    pl.semaphore_wait(row_sem, 1)
    group = 16

    def rotate(block, carry):
        others = [peer(group * block + i) for i in range(group)]
        for other in others:
            near = turned[lax.rem(other - places + passes, passes)]
            far = turned[lax.rem(other - places + 2 * passes - 1, passes)]
            ready[other] = pltpu.roll(jnp.where(tile_lane < LANES - within, near, far), within, 1)
        for other in others:
            pltpu.make_async_remote_copy(
                src_ref=ready.at[other], dst_ref=facing.at[pl.ds(pl.multiple_of(tile * here, tile), tile)],
                send_sem=face_send, recv_sem=face_recv, device_id=(1 - row, other, span), device_id_type=MESH,
            ).start()
        return carry

    lax.fori_loop(0, passes // group, rotate, 0)

    for copy in old_loads:
        copy.wait()

    def store_residual(j, mine, part):
        at = pl.ds(SLICE * j, SLICE)
        resid[at, :] = INV_DT * (mine - resid[at, :]) + part

    apply(even, store_residual)
    correct(resid, 0, 1.0, False)

    all_faced = pltpu.make_async_remote_copy(
        src_ref=facing, dst_ref=facing, send_sem=face_send, recv_sem=face_recv,
        device_id=(1 - row, here, span), device_id_type=MESH)
    all_faced.wait()

    for j in range(SLICES):
        block = facing[pl.ds(j, 25, stride=SLICES), :]
        block = jnp.concatenate([block, jnp.zeros((7, LANES), jnp.float32)], axis=0)
        for half, piece in enumerate(halves(block)):
            face_x[j // 4, pl.ds(32 * half, 32), pl.ds(LANES * (j % 4), LANES)] = piece
    for s in (0, 4, 1, 2, 3):
        image = jnp.dot(face_op[...], face_x[s], preferred_element_type=jnp.float32)
        image = image[0:SLICE] + image[SLICE : 2 * SLICE]
        for elem in range(4):
            at = pl.ds(SLICE * (4 * s + elem), SLICE)
            whole = resid[at, :] + image[:, LANES * elem : LANES * (elem + 1)]
            resid[at, :] = whole
            odd[at, :] = whole * (-1.0 / DIAG)
        if s == 4:
            span_copy(odd, 1).start()
    pack_up[1], pack_down[1] = packed(odd)
    for copy in pitch_copies(1):
        copy.start()

    def interleave(field, rows):
        flat_rows = rows.reshape(125 * SLICES, LANES)
        for j in range(SLICES):
            flat_rows[pl.ds(j, 125, stride=SLICES), :] = field[pl.ds(SLICE * j, 125), :]

    interleave(resid, resid_rows)
    rate = OMEGA / DIAG
    for t in range(1, SWEEPS + 1):
        field, after = values[t % 2], values[1 - t % 2]

        def store(j, mine, part):
            at = pl.ds(SLICE * j, SLICE)
            image = (INV_DT + INV_DTAU) * mine + part
            after[at, :] = mine - rate * (resid[at, :] + image)

        apply(field, store)
        correct(after, t, -rate, t < SWEEPS)
    interleave(values[(SWEEPS + 1) % 2], update_rows)


def write_kernel(resid, update, residual_out, update_out, sems):
    copies = [
        pltpu.make_async_copy(rows, out, sems.at[k])
        for k, (rows, out) in enumerate(((update, update_out), (resid, residual_out)))
    ]
    for copy in copies:
        copy.start()
    for copy in copies:
        copy.wait()


def per_device(passes, state, old_state, jacobians, offset):
    shape = state.shape
    tile = TRACE // passes
    in_hbm = pl.BlockSpec(memory_space=pltpu.HBM)
    f32, bf16, dma = jnp.float32, jnp.bfloat16, pltpu.SemaphoreType.DMA
    exchanges = SWEEPS + 1
    viewed = (125, SLICES, 1, LANES)
    pinned = lambda x: pltpu.with_memory_space_constraint(x, pltpu.HBM)
    in_vmem = pl.BlockSpec(memory_space=pltpu.VMEM)
    slices = (SLICE * SLICES + 40, LANES)
    fields = pl.pallas_call(
        functools.partial(kernel, passes),
        out_shape=[jax.ShapeDtypeStruct((625, 4, LANES), f32)] * 2,
        in_specs=[in_hbm, in_hbm, in_hbm, pl.BlockSpec(memory_space=pltpu.SMEM), in_hbm],
        out_specs=[in_vmem] * 2,
        scratch_shapes=[
            pltpu.VMEM(slices, f32),
            pltpu.VMEM(slices, f32),
            pltpu.VMEM(slices, f32),
            pltpu.VMEM((26, SLICES, 1, LANES), f32),
            pltpu.VMEM((passes, tile, LANES), f32),
            pltpu.VMEM((passes, tile, LANES), f32),
            pltpu.VMEM((TRACE, LANES), f32),
            pltpu.VMEM((13, SLICE, SLICE), f32),
            pltpu.VMEM((3, 8, LANES), f32),
            pltpu.VMEM((5, 3, 5), f32),
            pltpu.VMEM((SLICE + 32, LANES), f32),
            pltpu.VMEM((2 * SLICE, 5 * SLICE), bf16),
            pltpu.VMEM((2 * SLICE, 64), bf16),
            pltpu.VMEM((2 * SLICE, 2 * SLICE), bf16),
            pltpu.VMEM((128, 128), bf16),
            pltpu.VMEM((5, 5 * SLICE, 4 * LANES), bf16),
            pltpu.VMEM((5, 64, 4 * LANES), bf16),
            pltpu.VMEM((exchanges, 32, LANES), f32),
            pltpu.VMEM((exchanges, 32, LANES), f32),
            pltpu.VMEM((exchanges, 32, LANES), f32),
            pltpu.VMEM((exchanges, 32, LANES), f32),
            pltpu.VMEM((exchanges, SLICE, LANES), f32),
            dma((SLICES,)), dma((SLICES,)), dma((5,)), dma, dma,
            pltpu.SemaphoreType.REGULAR, dma, dma, dma, dma, dma((3, exchanges)), dma((3, exchanges)),
        ],
        compiler_params=pltpu.CompilerParams(
            collective_id=0, has_side_effects=True, vmem_limit_bytes=40 * 1024 * 1024
        ),
        name="pseudo_step",
    )(
        pinned(state.reshape(viewed)), pinned(old_state.reshape(viewed)),
        pinned(jnp.transpose(jacobians, (1, 0, 2))), offset, pinned(jnp.asarray(operator_patterns())),
    )
    outs = pl.pallas_call(
        write_kernel,
        out_shape=[jax.ShapeDtypeStruct((625, 4, LANES), f32)] * 2,
        in_specs=[pl.BlockSpec(memory_space=pl.ANY)] * 2,
        out_specs=[in_hbm] * 2,
        scratch_shapes=[dma((2,))],
        compiler_params=pltpu.CompilerParams(vmem_limit_bytes=1024 * 1024),
        name="write_fields",
    )(*fields)
    return tuple(out.reshape(shape) for out in outs)


def solution(mesh):
    placed = P("row", None, None, None, "span", "pass")
    return jax.shard_map(
        functools.partial(per_device, mesh.shape["pass"]),
        mesh=mesh,
        in_specs=(placed, placed, P(), P()),
        out_specs=(placed, placed),
        check_vma=False,
    )
```

```python
import functools
import math

import jax
import jax.numpy as jnp
import numpy as np
from jax import lax
from jax.experimental import pallas as pl
from jax.experimental.pallas import tpu as pltpu
from jax.sharding import PartitionSpec as P

SWEEPS = 3
LIFT_HALF = 5.0
INV_DT = 1.5
INV_DTAU = 1.0
DIAG = 12.0
OMEGA = 0.7

LANES = 128
SLICE = 128
SLICES = 20
TRACE = 512
MESH = pl.DeviceIdType.MESH
HIGHEST = lax.Precision.HIGHEST


def gll_derivative():
    nodes = np.array([-1.0, -math.sqrt(3.0 / 7.0), 0.0, math.sqrt(3.0 / 7.0), 1.0])
    legend = (35.0 * nodes**4 - 30.0 * nodes**2 + 3.0) / 8.0
    table = np.zeros((5, 5))
    for left in range(5):
        for right in range(5):
            if left != right:
                table[left, right] = legend[left] / (legend[right] * (nodes[left] - nodes[right]))
    return table


def operator_patterns():
    deriv = gll_derivative()
    planes = np.zeros((13, SLICE, SLICE), np.float32)
    places = [(v, a, p) for v in range(5) for a in range(5) for p in range(5)]
    for q, (v, a, p) in enumerate(places):
        planes[12, q, v] = 1.0
        planes[4, v, q] = 1.0
        planes[3, q, q] = LIFT_HALF * ((a in (0, 4)) + (p in (0, 4)))
        for c, (w, b, r) in enumerate(places):
            planes[0, q, c] = deriv[a, b] * (p == r)
            planes[1, q, c] = deriv[p, r] * (a == b)
            planes[2, q, c] = (a == b) * (p == r)
        for w in range(5):
            for k in range(5):
                low, high, face = 5 * w + k, 32 + 5 * w + k, 64 + 5 * w + k
                if p == 0 and a == k:
                    planes[7, q, low] = -LIFT_HALF
                    planes[8:10, q, low] = -LIFT_HALF * (v == w)
                if p == 4 and a == k:
                    planes[7, q, high] = LIFT_HALF
                    planes[8:10, q, high] = -LIFT_HALF * (v == w)
                if a == 4 and p == k:
                    planes[10, q, face] = LIFT_HALF
                    planes[8, q, face] = -LIFT_HALF * (v == w)
                if a == 0 and p == k:
                    planes[11, q, face] = -LIFT_HALF
                    planes[9, q, face] = -LIFT_HALF * (v == w)
    for w in range(5):
        planes[5, w, 5 * w : 5 * w + 5] = 1.0
        planes[5, w, 32 + 5 * w : 32 + 5 * w + 5] = 1.0
        planes[6, w, 64 + 5 * w : 64 + 5 * w + 5] = 1.0
    return planes


def send_order():
    far_z, far_y = (4, 3, 5, 2, 6, 1, 7, 0), (2, 1, 3, 0)
    return [(y, z, core) for core in (1, 0) for z in far_z for y in far_y]


def halves(x):
    high = x.astype(jnp.bfloat16)
    low = (x - high.astype(jnp.float32)).astype(jnp.bfloat16)
    return high, low


def kernel(
    passes,
    state, older, jacobians, offset, planes,
    resid_rows, update_rows,
    resid, even, odd, trace, turned, ready, facing, pats, spread, jacs, edge_rows,
    main_op, face_op, span_op, pitch_op, main_x, face_x,
    pack_up, pack_down, from_low, from_high, from_span,
    load_sem, old_sem, trace_sem, pat_sem, jac_sem,
    row_sem, turn_send, turn_recv, face_send, face_recv, halo_send, halo_recv,
):
    values = (even, odd)
    row, here, span = lax.axis_index("row"), lax.axis_index("pass"), lax.axis_index("span")
    up, down = lax.rem(here + 1, passes), lax.rem(here + passes - 1, passes)
    tile = TRACE // passes
    deriv = gll_derivative()

    order = send_order()

    def at(offset):
        y = lax.rem(here // 16 + offset[0], 4)
        z = lax.rem(here // 2 + offset[1], 8)
        return 16 * y + 2 * z + lax.rem(here + offset[2], 2)

    barrier = pltpu.get_barrier_semaphore()

    for offset_of in order[:-1]:
        pl.semaphore_signal(barrier, inc=1, device_id=(row, at(offset_of), span), device_id_type=MESH)
    pl.semaphore_signal(barrier, inc=1, device_id=(1 - row, here, span), device_id_type=MESH)
    pl.semaphore_signal(barrier, inc=1, device_id=(row, here, 1 - span), device_id_type=MESH)

    loads = [
        pltpu.make_async_copy(state.at[:, j, 0, :], even.at[pl.ds(SLICE * j, 125)], load_sem.at[j])
        for j in range(SLICES)
    ]
    old_loads = [
        pltpu.make_async_copy(older.at[:, j, 0, :], resid.at[pl.ds(SLICE * j, 125)], old_sem.at[j])
        for j in range(SLICES)
    ]
    plane_at = 20 * (1 - row)
    trace_loads = [
        pltpu.make_async_copy(
            state.at[pl.ds(25 * v + plane_at, 5)], trace.at[pl.ds(5 * v, 5)], trace_sem.at[v]
        )
        for v in range(5)
    ]
    pat_load = pltpu.make_async_copy(planes, pats, pat_sem)
    jac_load = pltpu.make_async_copy(jacobians, jacs, jac_sem)
    for copy in trace_loads + loads + [pat_load, jac_load] + old_loads:
        copy.start()

    lane = lax.broadcasted_iota(jnp.int32, (32, LANES), 1)
    sent = (SLICES - 1) * (1 - span)
    sent_rows = pl.ds(pl.multiple_of(SLICE * sent, SLICE), SLICE)

    def pitch_rows(field, j, node):
        return field[pl.ds(SLICE * j + node, 32, stride=5), :]

    def span_copy(field, t):
        return pltpu.make_async_remote_copy(
            src_ref=field.at[sent_rows], dst_ref=from_span.at[t],
            send_sem=halo_send.at[0, t], recv_sem=halo_recv.at[0, t],
            device_id=(row, here, 1 - span), device_id_type=MESH)

    def pitch_copies(t):
        return [
            pltpu.make_async_remote_copy(
                src_ref=pack_up.at[t], dst_ref=from_low.at[t],
                send_sem=halo_send.at[1, t], recv_sem=halo_recv.at[1, t],
                device_id=(row, up, span), device_id_type=MESH),
            pltpu.make_async_remote_copy(
                src_ref=pack_down.at[t], dst_ref=from_high.at[t],
                send_sem=halo_send.at[2, t], recv_sem=halo_recv.at[2, t],
                device_id=(row, down, span), device_id_type=MESH),
        ]

    def packed(field):
        upward = jnp.zeros((32, LANES), jnp.float32)
        downward = jnp.zeros((32, LANES), jnp.float32)
        for j in range(SLICES):
            upward = jnp.where(lane == j, pltpu.roll(pitch_rows(field, j, 4), j + 1, 1), upward)
            first = pitch_rows(field, j, 0)
            downward = jnp.where(lane == j, pltpu.roll(first, j, 1) if j else first, downward)
        return upward, downward

    def split_main(field, elem):
        cols = pl.ds(LANES * elem, LANES)

        def chunk(c, carry):
            at = pl.multiple_of(16 * c, 16)
            load = lambda j: field[pl.ds(pl.multiple_of(SLICE * j + at, 16), 16), :]
            v = [load(4 * s + elem) for s in range(5)]
            sum04, dif04, sum13, dif13 = v[0] + v[4], v[0] - v[4], v[1] + v[3], v[1] - v[3]
            d = lambda i, j: float(deriv[i, j])
            odd0 = (0.5 * (d(0, 1) + d(0, 3))) * sum13 + d(0, 2) * v[2] + (0.5 * d(0, 4)) * sum04
            even0 = (0.5 * (d(0, 1) - d(0, 3))) * dif13 - (0.5 * d(0, 4)) * dif04
            odd1 = (0.5 * (d(1, 0) + d(1, 4))) * sum04 + d(1, 2) * v[2] + (0.5 * d(1, 3)) * sum13
            even1 = (0.5 * (d(1, 0) - d(1, 4))) * dif04 - (0.5 * d(1, 3)) * dif13
            g = [
                even0 + odd0,
                even1 + odd1,
                d(2, 0) * dif04 + d(2, 1) * dif13,
                even1 - odd1,
                even0 - odd0,
            ]
            if elem > 0:
                g[0] = g[0] - LIFT_HALF * load(16 + elem - 1)
            if elem < 3:
                g[4] = g[4] + LIFT_HALF * load(elem + 1)
            for s in range(5):
                for part, block in enumerate((v[s], g[s])):
                    for half, piece in enumerate(halves(block)):
                        place = 2 * SLICE * half + SLICE * part
                        main_x[s, pl.ds(pl.multiple_of(place + at, 16), 16), cols] = piece
            return carry

        lax.fori_loop(0, SLICE // 16, chunk, 0)

    def split_ghosts(field):
        for j in range(SLICES):
            cols = pl.ds(LANES * (j % 4), LANES)
            low = jnp.where(lane == 0, 0.0, pltpu.roll(pitch_rows(field, j, 4), 1, 1))
            high = jnp.where(lane == LANES - 1, 0.0, pltpu.roll(pitch_rows(field, j, 0), LANES - 1, 1))
            for part, block in enumerate((low, high)):
                for half, piece in enumerate(halves(block)):
                    main_x[j // 4, pl.ds(4 * SLICE + 64 * half + 32 * part, 32), cols] = piece

    def apply(field, store):
        for elem in range(4):
            split_main(field, elem)
        split_ghosts(field)
        for s in range(5):
            image = jnp.dot(main_op[...], main_x[s], preferred_element_type=jnp.float32)
            image = image[0:SLICE] + image[SLICE : 2 * SLICE]
            for elem in range(4):
                j = 4 * s + elem
                mine = field[pl.ds(SLICE * j, SLICE), :]
                part = image[:, LANES * elem : LANES * (elem + 1)]
                if s in (0, 4):
                    jump = mine
                    if s == 0 and elem > 0:
                        jump = mine - field[pl.ds(SLICE * (16 + elem - 1), SLICE), :]
                    if s == 4 and elem < 3:
                        jump = mine - field[pl.ds(SLICE * (elem + 1), SLICE), :]
                    part = part + LIFT_HALF * jump
                store(j, mine, part)

    def correct(field, t, factor, send_on):
        if send_on:
            upward, downward = packed(field)
        for copy in pitch_copies(t):
            copy.wait()
        pieces = [piece for got in (from_low[t], from_high[t]) for piece in halves(got)]
        edge = jnp.dot(pitch_op[...], jnp.concatenate(pieces, 0), preferred_element_type=jnp.float32)
        low = factor * (edge[0:32] + edge[32:64])
        high = factor * (edge[64:96] + edge[96:128])
        span_copy(field, t).wait()
        share = jnp.dot(span_op[...], jnp.concatenate(halves(from_span[t]), 0), preferred_element_type=jnp.float32)
        field[sent_rows, :] = field[sent_rows, :] + factor * (share[0:SLICE] + share[SLICE : 2 * SLICE])

        def columns(j):
            at_low = pl.ds(SLICE * j, 25, stride=5)
            at_high = pl.ds(SLICE * j + 4, 25, stride=5)
            came = pltpu.roll(low, lax.rem(LANES - j, LANES), 1)
            field[at_low, :] = field[at_low, :] + jnp.where(lane == 0, came, 0.0)[0:25]
            came = pltpu.roll(high, LANES - 1 - j, 1)
            field[at_high, :] = field[at_high, :] + jnp.where(lane == LANES - 1, came, 0.0)[0:25]

        columns(sent)
        if send_on:
            span_copy(field, t + 1).start()
            last = pltpu.roll(pitch_rows(field, sent, 4), sent + 1, 1)
            first = pltpu.roll(pitch_rows(field, sent, 0), sent, 1)
            pack_up[t + 1] = jnp.where(lane == sent, last, upward + high)
            pack_down[t + 1] = jnp.where(lane == sent, first, downward + low)
            for copy in pitch_copies(t + 1):
                copy.start()
        columns(SLICES - 1 - sent)
        for j in range(1, SLICES - 1):
            columns(j)

    trace[pl.ds(25, 1)] = jnp.zeros((1, SLICES, 1, LANES), jnp.float32)
    for copy in trace_loads:
        copy.wait()
    pl.semaphore_wait(barrier, passes + 1)
    pl.semaphore_signal(row_sem, inc=1, device_id=(1 - row, here, span), device_id_type=MESH)
    flat = trace.reshape(26 * SLICES, LANES)

    def turn_copy(other):
        return pltpu.make_async_remote_copy(
            src_ref=flat.at[pl.ds(pl.multiple_of(tile * other, tile), tile)], dst_ref=turned.at[here],
            send_sem=turn_send, recv_sem=turn_recv, device_id=(row, other, span), device_id_type=MESH)

    for offset_of in order[:-1]:
        turn_copy(at(offset_of)).start()
    turned[here] = flat[pl.ds(pl.multiple_of(tile * here, tile), tile), :]

    for field in (even, resid):
        for j in range(SLICES):
            field[pl.ds(SLICE * j + 125, 3), :] = jnp.zeros((3, LANES), jnp.float32)
    for field in (even, odd):
        field[pl.ds(SLICE * SLICES, 40), :] = jnp.zeros((40, LANES), jnp.float32)

    pat_load.wait()
    jac_load.wait()
    spread[...] = jnp.zeros_like(spread)
    for d in range(3):
        spread[d, 0:5, 0:5] = jacs[:, d, :]
    rows = pats[12][:, 0:8]

    def spread_out(d, plane):
        by_row = jnp.dot(rows, spread[d], precision=HIGHEST, preferred_element_type=jnp.float32)
        return jnp.dot(by_row, pats[plane], precision=HIGHEST, preferred_element_type=jnp.float32)

    own = spread_out(0, 4) * pats[0] + spread_out(1, 4) * pats[1] + pats[3]
    along = spread_out(2, 4) * pats[2]
    edges = spread_out(1, 5) * pats[7] + spread_out(0, 6) * pats[10 + row] + pats[8 + row]
    for half in range(2):
        op_rows = pl.ds(SLICE * half, SLICE)
        for part, block in enumerate((own, along)):
            piece = halves(block)[half]
            for again in range(2):
                main_op[op_rows, pl.ds(2 * SLICE * again + SLICE * part, SLICE)] = piece
        piece = halves(edges)[half]
        for again in range(2):
            main_op[op_rows, pl.ds(4 * SLICE + 64 * again, 64)] = piece[:, 0:64]
            face_op[op_rows, pl.ds(32 * again, 32)] = piece[:, 64:96]
    square = (SLICE, SLICE)
    same = lax.broadcasted_iota(jnp.int32, square, 0) == lax.broadcasted_iota(jnp.int32, square, 1)
    outer = jnp.where(span == 0, LIFT_HALF, -LIFT_HALF) * along - jnp.where(same, LIFT_HALF, 0.0)
    edge_rows[pl.ds(0, SLICE), :] = edges
    edge_rows[pl.ds(SLICE, 32), :] = jnp.zeros((32, LANES), jnp.float32)
    lows = edge_rows[pl.ds(0, 32, stride=5), :][:, 0:32]
    highs = edge_rows[pl.ds(4, 32, stride=5), :][:, 32:64]
    pitch_op[...] = jnp.zeros_like(pitch_op)
    for half in range(2):
        for again in range(2):
            span_op[pl.ds(SLICE * half, SLICE), pl.ds(SLICE * again, SLICE)] = halves(outer)[half]
            pitch_op[pl.ds(32 * half, 32), pl.ds(32 * again, 32)] = halves(lows)[half]
            pitch_op[pl.ds(64 + 32 * half, 32), pl.ds(64 + 32 * again, 32)] = halves(highs)[half]

    for copy in loads:
        copy.wait()
    span_copy(even, 0).start()
    pack_up[0], pack_down[0] = packed(even)
    for copy in pitch_copies(0):
        copy.start()

    all_turned = pltpu.make_async_remote_copy(
        src_ref=turned.at[pl.ds(0, passes - 1)], dst_ref=turned.at[pl.ds(0, passes - 1)],
        send_sem=turn_send, recv_sem=turn_recv, device_id=(row, up, span), device_id_type=MESH)
    all_turned.wait()
    total = LANES * passes
    shift = lax.rem(lax.rem(offset[0], total) + total, total)
    shift = jnp.where(row == 0, shift, lax.rem(total - shift, total))
    places = shift // LANES
    within = lax.rem(shift, LANES)
    tile_lane = lax.broadcasted_iota(jnp.int32, (tile, LANES), 1)

    pl.semaphore_wait(row_sem, 1)
    group = 16

    def rotate(block):
        others = [at(order[group * block + i]) for i in range(group)]
        for other in others:
            near = turned[lax.rem(other - places + passes, passes)]
            far = turned[lax.rem(other - places + 2 * passes - 1, passes)]
            ready[other] = pltpu.roll(jnp.where(tile_lane < LANES - within, near, far), within, 1)
        for other in others:
            pltpu.make_async_remote_copy(
                src_ref=ready.at[other], dst_ref=facing.at[pl.ds(pl.multiple_of(tile * here, tile), tile)],
                send_sem=face_send, recv_sem=face_recv, device_id=(1 - row, other, span), device_id_type=MESH,
            ).start()

    for block in range(passes // group):
        rotate(block)

    for copy in old_loads:
        copy.wait()

    def store_residual(j, mine, part):
        at = pl.ds(SLICE * j, SLICE)
        resid[at, :] = INV_DT * (mine - resid[at, :]) + part

    apply(even, store_residual)
    correct(resid, 0, 1.0, False)

    all_faced = pltpu.make_async_remote_copy(
        src_ref=facing, dst_ref=facing, send_sem=face_send, recv_sem=face_recv,
        device_id=(1 - row, here, span), device_id_type=MESH)
    all_faced.wait()

    for j in range(SLICES):
        block = facing[pl.ds(j, 25, stride=SLICES), :]
        block = jnp.concatenate([block, jnp.zeros((7, LANES), jnp.float32)], axis=0)
        for half, piece in enumerate(halves(block)):
            face_x[j // 4, pl.ds(32 * half, 32), pl.ds(LANES * (j % 4), LANES)] = piece
    for s in (0, 4, 1, 2, 3):
        image = jnp.dot(face_op[...], face_x[s], preferred_element_type=jnp.float32)
        image = image[0:SLICE] + image[SLICE : 2 * SLICE]
        for elem in range(4):
            at = pl.ds(SLICE * (4 * s + elem), SLICE)
            whole = resid[at, :] + image[:, LANES * elem : LANES * (elem + 1)]
            resid[at, :] = whole
            odd[at, :] = whole * (-1.0 / DIAG)
        if s == 4:
            span_copy(odd, 1).start()
    pack_up[1], pack_down[1] = packed(odd)
    for copy in pitch_copies(1):
        copy.start()

    def interleave(field, rows):
        flat_rows = rows.reshape(125 * SLICES, LANES)
        for j in range(SLICES):
            flat_rows[pl.ds(j, 125, stride=SLICES), :] = field[pl.ds(SLICE * j, 125), :]

    interleave(resid, resid_rows)
    rate = OMEGA / DIAG
    for t in range(1, SWEEPS + 1):
        field, after = values[t % 2], values[1 - t % 2]

        def store(j, mine, part):
            at = pl.ds(SLICE * j, SLICE)
            image = (INV_DT + INV_DTAU) * mine + part
            after[at, :] = mine - rate * (resid[at, :] + image)

        apply(field, store)
        correct(after, t, -rate, t < SWEEPS)
    interleave(values[(SWEEPS + 1) % 2], update_rows)


def write_kernel(resid, update, residual_out, update_out, sems):
    copies = [
        pltpu.make_async_copy(rows, out, sems.at[k])
        for k, (rows, out) in enumerate(((update, update_out), (resid, residual_out)))
    ]
    for copy in copies:
        copy.start()
    for copy in copies:
        copy.wait()


def per_device(passes, state, old_state, jacobians, offset):
    shape = state.shape
    tile = TRACE // passes
    in_hbm = pl.BlockSpec(memory_space=pltpu.HBM)
    f32, bf16, dma = jnp.float32, jnp.bfloat16, pltpu.SemaphoreType.DMA
    exchanges = SWEEPS + 1
    viewed = (125, SLICES, 1, LANES)
    pinned = lambda x: pltpu.with_memory_space_constraint(x, pltpu.HBM)
    in_vmem = pl.BlockSpec(memory_space=pltpu.VMEM)
    slices = (SLICE * SLICES + 40, LANES)
    fields = pl.pallas_call(
        functools.partial(kernel, passes),
        out_shape=[jax.ShapeDtypeStruct((625, 4, LANES), f32)] * 2,
        in_specs=[in_hbm, in_hbm, in_hbm, pl.BlockSpec(memory_space=pltpu.SMEM), in_hbm],
        out_specs=[in_vmem] * 2,
        scratch_shapes=[
            pltpu.VMEM(slices, f32),
            pltpu.VMEM(slices, f32),
            pltpu.VMEM(slices, f32),
            pltpu.VMEM((26, SLICES, 1, LANES), f32),
            pltpu.VMEM((passes, tile, LANES), f32),
            pltpu.VMEM((passes, tile, LANES), f32),
            pltpu.VMEM((TRACE, LANES), f32),
            pltpu.VMEM((13, SLICE, SLICE), f32),
            pltpu.VMEM((3, 8, LANES), f32),
            pltpu.VMEM((5, 3, 5), f32),
            pltpu.VMEM((SLICE + 32, LANES), f32),
            pltpu.VMEM((2 * SLICE, 5 * SLICE), bf16),
            pltpu.VMEM((2 * SLICE, 64), bf16),
            pltpu.VMEM((2 * SLICE, 2 * SLICE), bf16),
            pltpu.VMEM((128, 128), bf16),
            pltpu.VMEM((5, 5 * SLICE, 4 * LANES), bf16),
            pltpu.VMEM((5, 64, 4 * LANES), bf16),
            pltpu.VMEM((exchanges, 32, LANES), f32),
            pltpu.VMEM((exchanges, 32, LANES), f32),
            pltpu.VMEM((exchanges, 32, LANES), f32),
            pltpu.VMEM((exchanges, 32, LANES), f32),
            pltpu.VMEM((exchanges, SLICE, LANES), f32),
            dma((SLICES,)), dma((SLICES,)), dma((5,)), dma, dma,
            pltpu.SemaphoreType.REGULAR, dma, dma, dma, dma, dma((3, exchanges)), dma((3, exchanges)),
        ],
        compiler_params=pltpu.CompilerParams(
            collective_id=0, has_side_effects=True, vmem_limit_bytes=40 * 1024 * 1024
        ),
        name="pseudo_step",
    )(
        pinned(state.reshape(viewed)), pinned(old_state.reshape(viewed)),
        pinned(jnp.transpose(jacobians, (1, 0, 2))), offset, pinned(jnp.asarray(operator_patterns())),
    )
    outs = pl.pallas_call(
        write_kernel,
        out_shape=[jax.ShapeDtypeStruct((625, 4, LANES), f32)] * 2,
        in_specs=[pl.BlockSpec(memory_space=pl.ANY)] * 2,
        out_specs=[in_hbm] * 2,
        scratch_shapes=[dma((2,))],
        compiler_params=pltpu.CompilerParams(vmem_limit_bytes=1024 * 1024),
        name="write_fields",
    )(*fields)
    return tuple(out.reshape(shape) for out in outs)


def solution(mesh):
    placed = P("row", None, None, None, "span", "pass")
    return jax.shard_map(
        functools.partial(per_device, mesh.shape["pass"]),
        mesh=mesh,
        in_specs=(placed, placed, P(), P()),
        out_specs=(placed, placed),
        check_vma=False,
    )
```

```python
import functools
import math

import jax
import jax.numpy as jnp
import numpy as np
from jax import lax
from jax.experimental import pallas as pl
from jax.experimental.pallas import tpu as pltpu
from jax.sharding import PartitionSpec as P

SWEEPS = 3
LIFT_HALF = 5.0
INV_DT = 1.5
INV_DTAU = 1.0
DIAG = 12.0
OMEGA = 0.7

LANES = 128
SLICE = 128
SLICES = 20
TRACE = 512
MESH = pl.DeviceIdType.MESH
HIGHEST = lax.Precision.HIGHEST


def gll_derivative():
    nodes = np.array([-1.0, -math.sqrt(3.0 / 7.0), 0.0, math.sqrt(3.0 / 7.0), 1.0])
    legend = (35.0 * nodes**4 - 30.0 * nodes**2 + 3.0) / 8.0
    table = np.zeros((5, 5))
    for left in range(5):
        for right in range(5):
            if left != right:
                table[left, right] = legend[left] / (legend[right] * (nodes[left] - nodes[right]))
    return table


def operator_patterns():
    deriv = gll_derivative()
    planes = np.zeros((13, SLICE, SLICE), np.float32)
    places = [(v, a, p) for v in range(5) for a in range(5) for p in range(5)]
    for q, (v, a, p) in enumerate(places):
        planes[12, q, v] = 1.0
        planes[4, v, q] = 1.0
        planes[3, q, q] = LIFT_HALF * ((a in (0, 4)) + (p in (0, 4)))
        for c, (w, b, r) in enumerate(places):
            planes[0, q, c] = deriv[a, b] * (p == r)
            planes[1, q, c] = deriv[p, r] * (a == b)
            planes[2, q, c] = (a == b) * (p == r)
        for w in range(5):
            for k in range(5):
                low, high, face = 5 * w + k, 32 + 5 * w + k, 64 + 5 * w + k
                if p == 0 and a == k:
                    planes[7, q, low] = -LIFT_HALF
                    planes[8:10, q, low] = -LIFT_HALF * (v == w)
                if p == 4 and a == k:
                    planes[7, q, high] = LIFT_HALF
                    planes[8:10, q, high] = -LIFT_HALF * (v == w)
                if a == 4 and p == k:
                    planes[10, q, face] = LIFT_HALF
                    planes[8, q, face] = -LIFT_HALF * (v == w)
                if a == 0 and p == k:
                    planes[11, q, face] = -LIFT_HALF
                    planes[9, q, face] = -LIFT_HALF * (v == w)
    for w in range(5):
        planes[5, w, 5 * w : 5 * w + 5] = 1.0
        planes[5, w, 32 + 5 * w : 32 + 5 * w + 5] = 1.0
        planes[6, w, 64 + 5 * w : 64 + 5 * w + 5] = 1.0
    return planes


def send_order():
    far_z, far_y = (4, 3, 5, 2, 6, 1, 7, 0), (2, 1, 3, 0)
    return [(y, z, core) for core in (1, 0) for z in far_z for y in far_y]


def halves(x):
    high = x.astype(jnp.bfloat16)
    low = (x - high.astype(jnp.float32)).astype(jnp.bfloat16)
    return high, low


def kernel(
    passes,
    state, older, jacobians, offset, planes,
    resid_rows, update_rows,
    resid, even, odd, trace, turned, ready, facing, pats, spread, jacs, edge_rows,
    main_op, face_op, span_op, pitch_op, main_x, face_x,
    pack_up, pack_down, from_low, from_high, from_span,
    load_sem, old_sem, trace_sem, pat_sem, jac_sem,
    row_sem, turn_send, turn_recv, face_send, face_recv, halo_send, halo_recv,
):
    values = (even, odd)
    row, here, span = lax.axis_index("row"), lax.axis_index("pass"), lax.axis_index("span")
    up, down = lax.rem(here + 1, passes), lax.rem(here + passes - 1, passes)
    tile = TRACE // passes
    deriv = gll_derivative()

    order = send_order()

    def at(offset):
        y = lax.rem(here // 16 + offset[0], 4)
        z = lax.rem(here // 2 + offset[1], 8)
        return 16 * y + 2 * z + lax.rem(here + offset[2], 2)

    barrier = pltpu.get_barrier_semaphore()

    for offset_of in order[:-1]:
        pl.semaphore_signal(barrier, inc=1, device_id=(row, at(offset_of), span), device_id_type=MESH)
    pl.semaphore_signal(barrier, inc=1, device_id=(1 - row, here, span), device_id_type=MESH)
    pl.semaphore_signal(barrier, inc=1, device_id=(row, here, 1 - span), device_id_type=MESH)

    loads = [
        pltpu.make_async_copy(state.at[:, j, 0, :], even.at[pl.ds(SLICE * j, 125)], load_sem.at[j])
        for j in range(SLICES)
    ]
    old_loads = [
        pltpu.make_async_copy(older.at[:, j, 0, :], resid.at[pl.ds(SLICE * j, 125)], old_sem.at[j])
        for j in range(SLICES)
    ]
    plane_at = 20 * (1 - row)
    trace_loads = [
        pltpu.make_async_copy(
            state.at[pl.ds(25 * v + plane_at, 5)], trace.at[pl.ds(5 * v, 5)], trace_sem.at[v]
        )
        for v in range(5)
    ]
    pat_load = pltpu.make_async_copy(planes, pats, pat_sem)
    jac_load = pltpu.make_async_copy(jacobians, jacs, jac_sem)
    for copy in trace_loads + loads + [pat_load, jac_load] + old_loads:
        copy.start()

    lane = lax.broadcasted_iota(jnp.int32, (32, LANES), 1)
    sent = (SLICES - 1) * (1 - span)
    sent_rows = pl.ds(pl.multiple_of(SLICE * sent, SLICE), SLICE)

    def pitch_rows(field, j, node):
        return field[pl.ds(SLICE * j + node, 32, stride=5), :]

    def span_copy(field, t):
        return pltpu.make_async_remote_copy(
            src_ref=field.at[sent_rows], dst_ref=from_span.at[t],
            send_sem=halo_send.at[0, t], recv_sem=halo_recv.at[0, t],
            device_id=(row, here, 1 - span), device_id_type=MESH)

    def pitch_copies(t):
        return [
            pltpu.make_async_remote_copy(
                src_ref=pack_up.at[t], dst_ref=from_low.at[t],
                send_sem=halo_send.at[1, t], recv_sem=halo_recv.at[1, t],
                device_id=(row, up, span), device_id_type=MESH),
            pltpu.make_async_remote_copy(
                src_ref=pack_down.at[t], dst_ref=from_high.at[t],
                send_sem=halo_send.at[2, t], recv_sem=halo_recv.at[2, t],
                device_id=(row, down, span), device_id_type=MESH),
        ]

    def packed(field):
        upward = jnp.zeros((32, LANES), jnp.float32)
        downward = jnp.zeros((32, LANES), jnp.float32)
        for j in range(SLICES):
            upward = jnp.where(lane == j, pltpu.roll(pitch_rows(field, j, 4), j + 1, 1), upward)
            first = pitch_rows(field, j, 0)
            downward = jnp.where(lane == j, pltpu.roll(first, j, 1) if j else first, downward)
        return upward, downward

    def split_main(field, elem):
        cols = pl.ds(LANES * elem, LANES)

        def chunk(c, carry):
            at = pl.multiple_of(16 * c, 16)
            load = lambda j: field[pl.ds(pl.multiple_of(SLICE * j + at, 16), 16), :]
            v = [load(4 * s + elem) for s in range(5)]
            sum04, dif04, sum13, dif13 = v[0] + v[4], v[0] - v[4], v[1] + v[3], v[1] - v[3]
            d = lambda i, j: float(deriv[i, j])
            odd0 = (0.5 * (d(0, 1) + d(0, 3))) * sum13 + d(0, 2) * v[2] + (0.5 * d(0, 4)) * sum04
            even0 = (0.5 * (d(0, 1) - d(0, 3))) * dif13 - (0.5 * d(0, 4)) * dif04
            odd1 = (0.5 * (d(1, 0) + d(1, 4))) * sum04 + d(1, 2) * v[2] + (0.5 * d(1, 3)) * sum13
            even1 = (0.5 * (d(1, 0) - d(1, 4))) * dif04 - (0.5 * d(1, 3)) * dif13
            g = [
                even0 + odd0,
                even1 + odd1,
                d(2, 0) * dif04 + d(2, 1) * dif13,
                even1 - odd1,
                even0 - odd0,
            ]
            if elem > 0:
                g[0] = g[0] - LIFT_HALF * load(16 + elem - 1)
            if elem < 3:
                g[4] = g[4] + LIFT_HALF * load(elem + 1)
            for s in range(5):
                for part, block in enumerate((v[s], g[s])):
                    for half, piece in enumerate(halves(block)):
                        place = 2 * SLICE * half + SLICE * part
                        main_x[s, pl.ds(pl.multiple_of(place + at, 16), 16), cols] = piece
            return carry

        lax.fori_loop(0, SLICE // 16, chunk, 0)

    def split_ghosts(field):
        for j in range(SLICES):
            cols = pl.ds(LANES * (j % 4), LANES)
            low = jnp.where(lane == 0, 0.0, pltpu.roll(pitch_rows(field, j, 4), 1, 1))
            high = jnp.where(lane == LANES - 1, 0.0, pltpu.roll(pitch_rows(field, j, 0), LANES - 1, 1))
            for part, block in enumerate((low, high)):
                for half, piece in enumerate(halves(block)):
                    main_x[j // 4, pl.ds(4 * SLICE + 64 * half + 32 * part, 32), cols] = piece

    def apply(field, store):
        for elem in range(4):
            split_main(field, elem)
        split_ghosts(field)
        for s in range(5):
            image = jnp.dot(main_op[...], main_x[s], preferred_element_type=jnp.float32)
            image = image[0:SLICE] + image[SLICE : 2 * SLICE]
            for elem in range(4):
                j = 4 * s + elem
                mine = field[pl.ds(SLICE * j, SLICE), :]
                part = image[:, LANES * elem : LANES * (elem + 1)]
                if s in (0, 4):
                    jump = mine
                    if s == 0 and elem > 0:
                        jump = mine - field[pl.ds(SLICE * (16 + elem - 1), SLICE), :]
                    if s == 4 and elem < 3:
                        jump = mine - field[pl.ds(SLICE * (elem + 1), SLICE), :]
                    part = part + LIFT_HALF * jump
                store(j, mine, part)

    def correct(field, t, factor, send_on):
        if send_on:
            upward, downward = packed(field)
        for copy in pitch_copies(t):
            copy.wait()
        pieces = [piece for got in (from_low[t], from_high[t]) for piece in halves(got)]
        edge = jnp.dot(pitch_op[...], jnp.concatenate(pieces, 0), preferred_element_type=jnp.float32)
        low = factor * (edge[0:32] + edge[32:64])
        high = factor * (edge[64:96] + edge[96:128])
        span_copy(field, t).wait()
        share = jnp.dot(span_op[...], jnp.concatenate(halves(from_span[t]), 0), preferred_element_type=jnp.float32)
        field[sent_rows, :] = field[sent_rows, :] + factor * (share[0:SLICE] + share[SLICE : 2 * SLICE])

        def columns(j):
            at_low = pl.ds(SLICE * j, 25, stride=5)
            at_high = pl.ds(SLICE * j + 4, 25, stride=5)
            came = pltpu.roll(low, lax.rem(LANES - j, LANES), 1)
            field[at_low, :] = field[at_low, :] + jnp.where(lane == 0, came, 0.0)[0:25]
            came = pltpu.roll(high, LANES - 1 - j, 1)
            field[at_high, :] = field[at_high, :] + jnp.where(lane == LANES - 1, came, 0.0)[0:25]

        columns(sent)
        if send_on:
            span_copy(field, t + 1).start()
            last = pltpu.roll(pitch_rows(field, sent, 4), sent + 1, 1)
            first = pltpu.roll(pitch_rows(field, sent, 0), sent, 1)
            pack_up[t + 1] = jnp.where(lane == sent, last, upward + high)
            pack_down[t + 1] = jnp.where(lane == sent, first, downward + low)
            for copy in pitch_copies(t + 1):
                copy.start()
        columns(SLICES - 1 - sent)
        for j in range(1, SLICES - 1):
            columns(j)

    trace[pl.ds(25, 1)] = jnp.zeros((1, SLICES, 1, LANES), jnp.float32)
    for copy in trace_loads:
        copy.wait()
    pl.semaphore_wait(barrier, passes + 1)
    pl.semaphore_signal(row_sem, inc=1, device_id=(1 - row, here, span), device_id_type=MESH)
    flat = trace.reshape(26 * SLICES, LANES)

    def turn_copy(other):
        return pltpu.make_async_remote_copy(
            src_ref=flat.at[pl.ds(pl.multiple_of(tile * other, tile), tile)], dst_ref=turned.at[here],
            send_sem=turn_send, recv_sem=turn_recv, device_id=(row, other, span), device_id_type=MESH)

    for offset_of in order[:-1]:
        turn_copy(at(offset_of)).start()
    turned[here] = flat[pl.ds(pl.multiple_of(tile * here, tile), tile), :]

    for field in (even, resid):
        for j in range(SLICES):
            field[pl.ds(SLICE * j + 125, 3), :] = jnp.zeros((3, LANES), jnp.float32)
    for field in (even, odd):
        field[pl.ds(SLICE * SLICES, 40), :] = jnp.zeros((40, LANES), jnp.float32)

    pat_load.wait()
    jac_load.wait()
    spread[...] = jnp.zeros_like(spread)
    for d in range(3):
        spread[d, 0:5, 0:5] = jacs[:, d, :]
    rows = pats[12][:, 0:8]

    def spread_out(d, plane):
        by_row = jnp.dot(rows, spread[d], precision=HIGHEST, preferred_element_type=jnp.float32)
        return jnp.dot(by_row, pats[plane], precision=HIGHEST, preferred_element_type=jnp.float32)

    own = spread_out(0, 4) * pats[0] + spread_out(1, 4) * pats[1] + pats[3]
    along = spread_out(2, 4) * pats[2]
    edges = spread_out(1, 5) * pats[7] + spread_out(0, 6) * pats[10 + row] + pats[8 + row]
    for half in range(2):
        op_rows = pl.ds(SLICE * half, SLICE)
        for part, block in enumerate((own, along)):
            piece = halves(block)[half]
            for again in range(2):
                main_op[op_rows, pl.ds(2 * SLICE * again + SLICE * part, SLICE)] = piece
        piece = halves(edges)[half]
        for again in range(2):
            main_op[op_rows, pl.ds(4 * SLICE + 64 * again, 64)] = piece[:, 0:64]
            face_op[op_rows, pl.ds(32 * again, 32)] = piece[:, 64:96]
    square = (SLICE, SLICE)
    same = lax.broadcasted_iota(jnp.int32, square, 0) == lax.broadcasted_iota(jnp.int32, square, 1)
    outer = jnp.where(span == 0, LIFT_HALF, -LIFT_HALF) * along - jnp.where(same, LIFT_HALF, 0.0)
    edge_rows[pl.ds(0, SLICE), :] = edges
    edge_rows[pl.ds(SLICE, 32), :] = jnp.zeros((32, LANES), jnp.float32)
    lows = edge_rows[pl.ds(0, 32, stride=5), :][:, 0:32]
    highs = edge_rows[pl.ds(4, 32, stride=5), :][:, 32:64]
    pitch_op[...] = jnp.zeros_like(pitch_op)
    for half in range(2):
        for again in range(2):
            span_op[pl.ds(SLICE * half, SLICE), pl.ds(SLICE * again, SLICE)] = halves(outer)[half]
            pitch_op[pl.ds(32 * half, 32), pl.ds(32 * again, 32)] = halves(lows)[half]
            pitch_op[pl.ds(64 + 32 * half, 32), pl.ds(64 + 32 * again, 32)] = halves(highs)[half]

    for copy in loads:
        copy.wait()
    span_copy(even, 0).start()
    pack_up[0], pack_down[0] = packed(even)
    for copy in pitch_copies(0):
        copy.start()

    all_turned = pltpu.make_async_remote_copy(
        src_ref=turned.at[pl.ds(0, passes - 1)], dst_ref=turned.at[pl.ds(0, passes - 1)],
        send_sem=turn_send, recv_sem=turn_recv, device_id=(row, up, span), device_id_type=MESH)
    all_turned.wait()
    total = LANES * passes
    shift = lax.rem(lax.rem(offset[0], total) + total, total)
    shift = jnp.where(row == 0, shift, lax.rem(total - shift, total))
    places = shift // LANES
    within = lax.rem(shift, LANES)
    tile_lane = lax.broadcasted_iota(jnp.int32, (tile, LANES), 1)

    pl.semaphore_wait(row_sem, 1)
    group = 16

    def rotate(block):
        others = [at(order[group * block + i]) for i in range(group)]
        for other in others:
            near = turned[lax.rem(other - places + passes, passes)]
            far = turned[lax.rem(other - places + 2 * passes - 1, passes)]
            ready[other] = pltpu.roll(jnp.where(tile_lane < LANES - within, near, far), within, 1)
        for other in others:
            pltpu.make_async_remote_copy(
                src_ref=ready.at[other], dst_ref=facing.at[pl.ds(pl.multiple_of(tile * here, tile), tile)],
                send_sem=face_send, recv_sem=face_recv, device_id=(1 - row, other, span), device_id_type=MESH,
            ).start()

    for block in range(passes // group):
        rotate(block)

    for copy in old_loads:
        copy.wait()

    def store_residual(j, mine, part):
        at = pl.ds(SLICE * j, SLICE)
        resid[at, :] = INV_DT * (mine - resid[at, :]) + part

    apply(even, store_residual)
    correct(resid, 0, 1.0, False)

    all_faced = pltpu.make_async_remote_copy(
        src_ref=facing.at[pl.ds(0, TRACE)], dst_ref=facing.at[pl.ds(0, TRACE)], send_sem=face_send, recv_sem=face_recv,
        device_id=(1 - row, here, span), device_id_type=MESH)
    all_faced.wait()

    for j in range(SLICES):
        block = facing[pl.ds(j, 25, stride=SLICES), :]
        block = jnp.concatenate([block, jnp.zeros((7, LANES), jnp.float32)], axis=0)
        for half, piece in enumerate(halves(block)):
            face_x[j // 4, pl.ds(32 * half, 32), pl.ds(LANES * (j % 4), LANES)] = piece
    for s in (0, 4, 1, 2, 3):
        image = jnp.dot(face_op[...], face_x[s], preferred_element_type=jnp.float32)
        image = image[0:SLICE] + image[SLICE : 2 * SLICE]
        for elem in range(4):
            at = pl.ds(SLICE * (4 * s + elem), SLICE)
            whole = resid[at, :] + image[:, LANES * elem : LANES * (elem + 1)]
            resid[at, :] = whole
            odd[at, :] = whole * (-1.0 / DIAG)
        if s == 4:
            span_copy(odd, 1).start()
    pack_up[1], pack_down[1] = packed(odd)
    for copy in pitch_copies(1):
        copy.start()

    def interleave(field, rows):
        flat_rows = rows.reshape(125 * SLICES, LANES)
        for j in range(SLICES):
            flat_rows[pl.ds(j, 120, stride=SLICES), :] = field[pl.ds(SLICE * j, 120), :]
            flat_rows[pl.ds(j + 117 * SLICES, 8, stride=SLICES), :] = field[pl.ds(SLICE * j + 117, 8), :]

    interleave(resid, resid_rows)
    rate = OMEGA / DIAG
    for t in range(1, SWEEPS + 1):
        field, after = values[t % 2], values[1 - t % 2]

        def store(j, mine, part):
            at = pl.ds(SLICE * j, SLICE)
            image = (INV_DT + INV_DTAU) * mine + part
            after[at, :] = mine - rate * (resid[at, :] + image)

        apply(field, store)
        correct(after, t, -rate, t < SWEEPS)
    interleave(values[(SWEEPS + 1) % 2], update_rows)


def write_kernel(resid, update, residual_out, update_out, sems):
    copies = [
        pltpu.make_async_copy(rows, out, sems.at[k])
        for k, (rows, out) in enumerate(((update, update_out), (resid, residual_out)))
    ]
    for copy in copies:
        copy.start()
    for copy in copies:
        copy.wait()


def per_device(passes, state, old_state, jacobians, offset):
    shape = state.shape
    tile = TRACE // passes
    in_hbm = pl.BlockSpec(memory_space=pltpu.HBM)
    f32, bf16, dma = jnp.float32, jnp.bfloat16, pltpu.SemaphoreType.DMA
    exchanges = SWEEPS + 1
    viewed = (125, SLICES, 1, LANES)
    pinned = lambda x: pltpu.with_memory_space_constraint(x, pltpu.HBM)
    in_vmem = pl.BlockSpec(memory_space=pltpu.VMEM)
    slices = (SLICE * SLICES + 40, LANES)
    fields = pl.pallas_call(
        functools.partial(kernel, passes),
        out_shape=[jax.ShapeDtypeStruct((625, 4, LANES), f32)] * 2,
        in_specs=[in_hbm, in_hbm, in_hbm, pl.BlockSpec(memory_space=pltpu.SMEM), in_hbm],
        out_specs=[in_vmem] * 2,
        scratch_shapes=[
            pltpu.VMEM(slices, f32),
            pltpu.VMEM(slices, f32),
            pltpu.VMEM(slices, f32),
            pltpu.VMEM((26, SLICES, 1, LANES), f32),
            pltpu.VMEM((passes, tile, LANES), f32),
            pltpu.VMEM((passes, tile, LANES), f32),
            pltpu.VMEM((TRACE + LANES, LANES), f32),
            pltpu.VMEM((13, SLICE, SLICE), f32),
            pltpu.VMEM((3, 8, LANES), f32),
            pltpu.VMEM((5, 3, 5), f32),
            pltpu.VMEM((SLICE + 32, LANES), f32),
            pltpu.VMEM((2 * SLICE, 5 * SLICE), bf16),
            pltpu.VMEM((2 * SLICE, 64), bf16),
            pltpu.VMEM((2 * SLICE, 2 * SLICE), bf16),
            pltpu.VMEM((128, 128), bf16),
            pltpu.VMEM((5, 5 * SLICE, 4 * LANES), bf16),
            pltpu.VMEM((5, 64, 4 * LANES), bf16),
            pltpu.VMEM((exchanges, 32, LANES), f32),
            pltpu.VMEM((exchanges, 32, LANES), f32),
            pltpu.VMEM((exchanges, 32, LANES), f32),
            pltpu.VMEM((exchanges, 32, LANES), f32),
            pltpu.VMEM((exchanges, SLICE, LANES), f32),
            dma((SLICES,)), dma((SLICES,)), dma((5,)), dma, dma,
            pltpu.SemaphoreType.REGULAR, dma, dma, dma, dma, dma((3, exchanges)), dma((3, exchanges)),
        ],
        compiler_params=pltpu.CompilerParams(
            collective_id=0, has_side_effects=True, vmem_limit_bytes=40 * 1024 * 1024
        ),
        name="pseudo_step",
    )(
        pinned(state.reshape(viewed)), pinned(old_state.reshape(viewed)),
        pinned(jnp.transpose(jacobians, (1, 0, 2))), offset, pinned(jnp.asarray(operator_patterns())),
    )
    outs = pl.pallas_call(
        write_kernel,
        out_shape=[jax.ShapeDtypeStruct((625, 4, LANES), f32)] * 2,
        in_specs=[pl.BlockSpec(memory_space=pl.ANY)] * 2,
        out_specs=[in_hbm] * 2,
        scratch_shapes=[dma((2,))],
        compiler_params=pltpu.CompilerParams(vmem_limit_bytes=1024 * 1024),
        name="write_fields",
    )(*fields)
    return tuple(out.reshape(shape) for out in outs)


def solution(mesh):
    placed = P("row", None, None, None, "span", "pass")
    return jax.shard_map(
        functools.partial(per_device, mesh.shape["pass"]),
        mesh=mesh,
        in_specs=(placed, placed, P(), P()),
        out_specs=(placed, placed),
        check_vma=False,
    )
```

```python
import functools
import math

import jax
import jax.numpy as jnp
import numpy as np
from jax import lax
from jax.experimental import pallas as pl
from jax.experimental.pallas import tpu as pltpu
from jax.sharding import PartitionSpec as P

SWEEPS = 3
LIFT_HALF = 5.0
INV_DT = 1.5
INV_DTAU = 1.0
DIAG = 12.0
OMEGA = 0.7

LANES = 128
SLICE = 128
SLICES = 20
TRACE = 512
MESH = pl.DeviceIdType.MESH
HIGHEST = lax.Precision.HIGHEST


def gll_derivative():
    nodes = np.array([-1.0, -math.sqrt(3.0 / 7.0), 0.0, math.sqrt(3.0 / 7.0), 1.0])
    legend = (35.0 * nodes**4 - 30.0 * nodes**2 + 3.0) / 8.0
    table = np.zeros((5, 5))
    for left in range(5):
        for right in range(5):
            if left != right:
                table[left, right] = legend[left] / (legend[right] * (nodes[left] - nodes[right]))
    return table


def operator_patterns():
    deriv = gll_derivative()
    planes = np.zeros((13, SLICE, SLICE), np.float32)
    places = [(v, a, p) for v in range(5) for a in range(5) for p in range(5)]
    for q, (v, a, p) in enumerate(places):
        planes[12, q, v] = 1.0
        planes[4, v, q] = 1.0
        planes[3, q, q] = LIFT_HALF * ((a in (0, 4)) + (p in (0, 4)))
        for c, (w, b, r) in enumerate(places):
            planes[0, q, c] = deriv[a, b] * (p == r)
            planes[1, q, c] = deriv[p, r] * (a == b)
            planes[2, q, c] = (a == b) * (p == r)
        for w in range(5):
            for k in range(5):
                low, high, face = 5 * w + k, 32 + 5 * w + k, 64 + 5 * w + k
                if p == 0 and a == k:
                    planes[7, q, low] = -LIFT_HALF
                    planes[8:10, q, low] = -LIFT_HALF * (v == w)
                if p == 4 and a == k:
                    planes[7, q, high] = LIFT_HALF
                    planes[8:10, q, high] = -LIFT_HALF * (v == w)
                if a == 4 and p == k:
                    planes[10, q, face] = LIFT_HALF
                    planes[8, q, face] = -LIFT_HALF * (v == w)
                if a == 0 and p == k:
                    planes[11, q, face] = -LIFT_HALF
                    planes[9, q, face] = -LIFT_HALF * (v == w)
    for w in range(5):
        planes[5, w, 5 * w : 5 * w + 5] = 1.0
        planes[5, w, 32 + 5 * w : 32 + 5 * w + 5] = 1.0
        planes[6, w, 64 + 5 * w : 64 + 5 * w + 5] = 1.0
    return planes


def send_order():
    far_z, far_y = (4, 3, 5, 2, 6, 1, 7, 0), (2, 1, 3, 0)
    return [(y, z, core) for core in (1, 0) for z in far_z for y in far_y]


def halves(x):
    high = x.astype(jnp.bfloat16)
    low = (x - high.astype(jnp.float32)).astype(jnp.bfloat16)
    return high, low


def kernel(
    passes,
    state, older, jacobians, offset, planes,
    resid_rows, update_rows,
    resid, even, odd, trace, turned, ready, facing, pats, spread, jacs, edge_rows,
    main_op, face_op, span_op, pitch_op, main_x, face_x,
    pack_up, pack_down, from_low, from_high, from_span,
    load_sem, old_sem, trace_sem, pat_sem, jac_sem,
    row_sem, turn_send, turn_recv, face_send, face_recv, halo_send, halo_recv,
):
    values = (even, odd)
    row, here, span = lax.axis_index("row"), lax.axis_index("pass"), lax.axis_index("span")
    up, down = lax.rem(here + 1, passes), lax.rem(here + passes - 1, passes)
    tile = TRACE // passes
    deriv = gll_derivative()

    order = send_order()

    def at(offset):
        y = lax.rem(here // 16 + offset[0], 4)
        z = lax.rem(here // 2 + offset[1], 8)
        return 16 * y + 2 * z + lax.rem(here + offset[2], 2)

    barrier = pltpu.get_barrier_semaphore()

    for offset_of in order[:-1]:
        pl.semaphore_signal(barrier, inc=1, device_id=(row, at(offset_of), span), device_id_type=MESH)
    pl.semaphore_signal(barrier, inc=1, device_id=(1 - row, here, span), device_id_type=MESH)
    pl.semaphore_signal(barrier, inc=1, device_id=(row, here, 1 - span), device_id_type=MESH)

    loads = [
        pltpu.make_async_copy(state.at[:, j, 0, :], even.at[pl.ds(SLICE * j, 125)], load_sem.at[j])
        for j in range(SLICES)
    ]
    old_loads = [
        pltpu.make_async_copy(older.at[:, j, 0, :], resid.at[pl.ds(SLICE * j, 125)], old_sem.at[j])
        for j in range(SLICES)
    ]
    plane_at = 20 * (1 - row)
    trace_loads = [
        pltpu.make_async_copy(
            state.at[pl.ds(25 * v + plane_at, 5)], trace.at[pl.ds(5 * v, 5)], trace_sem.at[v]
        )
        for v in range(5)
    ]
    pat_load = pltpu.make_async_copy(planes, pats, pat_sem)
    jac_load = pltpu.make_async_copy(jacobians, jacs, jac_sem)
    for copy in trace_loads + loads + [pat_load, jac_load] + old_loads:
        copy.start()

    lane = lax.broadcasted_iota(jnp.int32, (32, LANES), 1)
    sent = (SLICES - 1) * (1 - span)
    sent_rows = pl.ds(pl.multiple_of(SLICE * sent, SLICE), SLICE)

    def pitch_rows(field, j, node):
        return field[pl.ds(SLICE * j + node, 32, stride=5), :]

    def span_copy(field, t):
        return pltpu.make_async_remote_copy(
            src_ref=field.at[sent_rows], dst_ref=from_span.at[t],
            send_sem=halo_send.at[0, t], recv_sem=halo_recv.at[0, t],
            device_id=(row, here, 1 - span), device_id_type=MESH)

    def pitch_copies(t):
        return [
            pltpu.make_async_remote_copy(
                src_ref=pack_up.at[t], dst_ref=from_low.at[t],
                send_sem=halo_send.at[1, t], recv_sem=halo_recv.at[1, t],
                device_id=(row, up, span), device_id_type=MESH),
            pltpu.make_async_remote_copy(
                src_ref=pack_down.at[t], dst_ref=from_high.at[t],
                send_sem=halo_send.at[2, t], recv_sem=halo_recv.at[2, t],
                device_id=(row, down, span), device_id_type=MESH),
        ]

    def packed(field):
        upward = jnp.zeros((32, LANES), jnp.float32)
        downward = jnp.zeros((32, LANES), jnp.float32)
        for j in range(SLICES):
            upward = jnp.where(lane == j, pltpu.roll(pitch_rows(field, j, 4), j + 1, 1), upward)
            first = pitch_rows(field, j, 0)
            downward = jnp.where(lane == j, pltpu.roll(first, j, 1) if j else first, downward)
        return upward, downward

    def split_main(field, elem):
        cols = pl.ds(LANES * elem, LANES)

        def chunk(c, carry):
            at = pl.multiple_of(16 * c, 16)
            load = lambda j: field[pl.ds(pl.multiple_of(SLICE * j + at, 16), 16), :]
            v = [load(4 * s + elem) for s in range(5)]
            sum04, dif04, sum13, dif13 = v[0] + v[4], v[0] - v[4], v[1] + v[3], v[1] - v[3]
            d = lambda i, j: float(deriv[i, j])
            odd0 = (0.5 * (d(0, 1) + d(0, 3))) * sum13 + d(0, 2) * v[2] + (0.5 * d(0, 4)) * sum04
            even0 = (0.5 * (d(0, 1) - d(0, 3))) * dif13 - (0.5 * d(0, 4)) * dif04
            odd1 = (0.5 * (d(1, 0) + d(1, 4))) * sum04 + d(1, 2) * v[2] + (0.5 * d(1, 3)) * sum13
            even1 = (0.5 * (d(1, 0) - d(1, 4))) * dif04 - (0.5 * d(1, 3)) * dif13
            g = [
                even0 + odd0,
                even1 + odd1,
                d(2, 0) * dif04 + d(2, 1) * dif13,
                even1 - odd1,
                even0 - odd0,
            ]
            if elem > 0:
                g[0] = g[0] - LIFT_HALF * load(16 + elem - 1)
            if elem < 3:
                g[4] = g[4] + LIFT_HALF * load(elem + 1)
            for s in range(5):
                for part, block in enumerate((v[s], g[s])):
                    for half, piece in enumerate(halves(block)):
                        place = 2 * SLICE * half + SLICE * part
                        main_x[s, pl.ds(pl.multiple_of(place + at, 16), 16), cols] = piece
            return carry

        lax.fori_loop(0, SLICE // 16, chunk, 0)

    def split_ghosts(field):
        for j in range(SLICES):
            cols = pl.ds(LANES * (j % 4), LANES)
            low = jnp.where(lane == 0, 0.0, pltpu.roll(pitch_rows(field, j, 4), 1, 1))
            high = jnp.where(lane == LANES - 1, 0.0, pltpu.roll(pitch_rows(field, j, 0), LANES - 1, 1))
            for part, block in enumerate((low, high)):
                for half, piece in enumerate(halves(block)):
                    main_x[j // 4, pl.ds(4 * SLICE + 64 * half + 32 * part, 32), cols] = piece

    def apply(field, store):
        for elem in range(4):
            split_main(field, elem)
        split_ghosts(field)
        for s in range(5):
            image = jnp.dot(main_op[...], main_x[s], preferred_element_type=jnp.float32)
            image = image[0:SLICE] + image[SLICE : 2 * SLICE]
            for elem in range(4):
                j = 4 * s + elem
                mine = field[pl.ds(SLICE * j, SLICE), :]
                part = image[:, LANES * elem : LANES * (elem + 1)]
                if s in (0, 4):
                    jump = mine
                    if s == 0 and elem > 0:
                        jump = mine - field[pl.ds(SLICE * (16 + elem - 1), SLICE), :]
                    if s == 4 and elem < 3:
                        jump = mine - field[pl.ds(SLICE * (elem + 1), SLICE), :]
                    part = part + LIFT_HALF * jump
                store(j, mine, part)

    def correct(field, t, factor, send_on):
        if send_on:
            upward, downward = packed(field)
        for copy in pitch_copies(t):
            copy.wait()
        pieces = [piece for got in (from_low[t], from_high[t]) for piece in halves(got)]
        edge = jnp.dot(pitch_op[...], jnp.concatenate(pieces, 0), preferred_element_type=jnp.float32)
        low = factor * (edge[0:32] + edge[32:64])
        high = factor * (edge[64:96] + edge[96:128])
        span_copy(field, t).wait()
        share = jnp.dot(span_op[...], jnp.concatenate(halves(from_span[t]), 0), preferred_element_type=jnp.float32)
        field[sent_rows, :] = field[sent_rows, :] + factor * (share[0:SLICE] + share[SLICE : 2 * SLICE])

        def columns(j):
            at_low = pl.ds(SLICE * j, 25, stride=5)
            at_high = pl.ds(SLICE * j + 4, 25, stride=5)
            came = pltpu.roll(low, lax.rem(LANES - j, LANES), 1)
            field[at_low, :] = field[at_low, :] + jnp.where(lane == 0, came, 0.0)[0:25]
            came = pltpu.roll(high, LANES - 1 - j, 1)
            field[at_high, :] = field[at_high, :] + jnp.where(lane == LANES - 1, came, 0.0)[0:25]

        columns(sent)
        if send_on:
            span_copy(field, t + 1).start()
            last = pltpu.roll(pitch_rows(field, sent, 4), sent + 1, 1)
            first = pltpu.roll(pitch_rows(field, sent, 0), sent, 1)
            pack_up[t + 1] = jnp.where(lane == sent, last, upward + high)
            pack_down[t + 1] = jnp.where(lane == sent, first, downward + low)
            for copy in pitch_copies(t + 1):
                copy.start()
        columns(SLICES - 1 - sent)
        for j in range(1, SLICES - 1):
            columns(j)

    trace[pl.ds(25, 1)] = jnp.zeros((1, SLICES, 1, LANES), jnp.float32)
    for copy in trace_loads:
        copy.wait()
    pl.semaphore_wait(barrier, passes + 1)
    pl.semaphore_signal(row_sem, inc=1, device_id=(1 - row, here, span), device_id_type=MESH)
    flat = trace.reshape(26 * SLICES, LANES)

    def turn_copy(other):
        return pltpu.make_async_remote_copy(
            src_ref=flat.at[pl.ds(pl.multiple_of(tile * other, tile), tile)], dst_ref=turned.at[here],
            send_sem=turn_send, recv_sem=turn_recv, device_id=(row, other, span), device_id_type=MESH)

    for offset_of in order[:-1]:
        turn_copy(at(offset_of)).start()
    turned[here] = flat[pl.ds(pl.multiple_of(tile * here, tile), tile), :]

    for field in (even, resid):
        for j in range(SLICES):
            field[pl.ds(SLICE * j + 125, 3), :] = jnp.zeros((3, LANES), jnp.float32)
    for field in (even, odd):
        field[pl.ds(SLICE * SLICES, 40), :] = jnp.zeros((40, LANES), jnp.float32)

    pat_load.wait()
    jac_load.wait()
    spread[...] = jnp.zeros_like(spread)
    for d in range(3):
        spread[d, 0:5, 0:5] = jacs[:, d, :]
    rows = pats[12][:, 0:8]

    def spread_out(d, plane):
        by_row = jnp.dot(rows, spread[d], precision=HIGHEST, preferred_element_type=jnp.float32)
        return jnp.dot(by_row, pats[plane], precision=HIGHEST, preferred_element_type=jnp.float32)

    own = spread_out(0, 4) * pats[0] + spread_out(1, 4) * pats[1] + pats[3]
    along = spread_out(2, 4) * pats[2]
    edges = spread_out(1, 5) * pats[7] + spread_out(0, 6) * pats[10 + row] + pats[8 + row]
    for half in range(2):
        op_rows = pl.ds(SLICE * half, SLICE)
        for part, block in enumerate((own, along)):
            piece = halves(block)[half]
            for again in range(2):
                main_op[op_rows, pl.ds(2 * SLICE * again + SLICE * part, SLICE)] = piece
        piece = halves(edges)[half]
        for again in range(2):
            main_op[op_rows, pl.ds(4 * SLICE + 64 * again, 64)] = piece[:, 0:64]
            face_op[op_rows, pl.ds(32 * again, 32)] = piece[:, 64:96]
    square = (SLICE, SLICE)
    same = lax.broadcasted_iota(jnp.int32, square, 0) == lax.broadcasted_iota(jnp.int32, square, 1)
    outer = jnp.where(span == 0, LIFT_HALF, -LIFT_HALF) * along - jnp.where(same, LIFT_HALF, 0.0)
    edge_rows[pl.ds(0, SLICE), :] = edges
    edge_rows[pl.ds(SLICE, 32), :] = jnp.zeros((32, LANES), jnp.float32)
    lows = edge_rows[pl.ds(0, 32, stride=5), :][:, 0:32]
    highs = edge_rows[pl.ds(4, 32, stride=5), :][:, 32:64]
    pitch_op[...] = jnp.zeros_like(pitch_op)
    for half in range(2):
        for again in range(2):
            span_op[pl.ds(SLICE * half, SLICE), pl.ds(SLICE * again, SLICE)] = halves(outer)[half]
            pitch_op[pl.ds(32 * half, 32), pl.ds(32 * again, 32)] = halves(lows)[half]
            pitch_op[pl.ds(64 + 32 * half, 32), pl.ds(64 + 32 * again, 32)] = halves(highs)[half]

    for copy in loads:
        copy.wait()
    span_copy(even, 0).start()
    pack_up[0], pack_down[0] = packed(even)
    for copy in pitch_copies(0):
        copy.start()

    all_turned = pltpu.make_async_remote_copy(
        src_ref=turned.at[pl.ds(0, passes - 1)], dst_ref=turned.at[pl.ds(0, passes - 1)],
        send_sem=turn_send, recv_sem=turn_recv, device_id=(row, up, span), device_id_type=MESH)
    all_turned.wait()
    total = LANES * passes
    shift = lax.rem(lax.rem(offset[0], total) + total, total)
    shift = jnp.where(row == 0, shift, lax.rem(total - shift, total))
    places = shift // LANES
    within = lax.rem(shift, LANES)
    tile_lane = lax.broadcasted_iota(jnp.int32, (tile, LANES), 1)

    pl.semaphore_wait(row_sem, 1)
    group = 8

    def rotate(block):
        others = [at(order[group * block + i]) for i in range(group)]
        for other in others:
            near = turned[lax.rem(other - places + passes, passes)]
            far = turned[lax.rem(other - places + 2 * passes - 1, passes)]
            ready[other] = pltpu.roll(jnp.where(tile_lane < LANES - within, near, far), within, 1)
        for other in others:
            pltpu.make_async_remote_copy(
                src_ref=ready.at[other], dst_ref=facing.at[pl.ds(pl.multiple_of(tile * here, tile), tile)],
                send_sem=face_send, recv_sem=face_recv, device_id=(1 - row, other, span), device_id_type=MESH,
            ).start()

    for block in range(passes // group):
        rotate(block)

    for copy in old_loads:
        copy.wait()

    def store_residual(j, mine, part):
        at = pl.ds(SLICE * j, SLICE)
        resid[at, :] = INV_DT * (mine - resid[at, :]) + part

    apply(even, store_residual)
    correct(resid, 0, 1.0, False)

    all_faced = pltpu.make_async_remote_copy(
        src_ref=facing.at[pl.ds(0, TRACE)], dst_ref=facing.at[pl.ds(0, TRACE)], send_sem=face_send, recv_sem=face_recv,
        device_id=(1 - row, here, span), device_id_type=MESH)
    all_faced.wait()

    for s in (0, 4, 1, 2, 3):
        for j in range(4 * s, 4 * s + 4):
            block = facing[pl.ds(j, 25, stride=SLICES), :]
            block = jnp.concatenate([block, jnp.zeros((7, LANES), jnp.float32)], axis=0)
            for half, piece in enumerate(halves(block)):
                face_x[j // 4, pl.ds(32 * half, 32), pl.ds(LANES * (j % 4), LANES)] = piece
        image = jnp.dot(face_op[...], face_x[s], preferred_element_type=jnp.float32)
        image = image[0:SLICE] + image[SLICE : 2 * SLICE]
        for elem in range(4):
            at = pl.ds(SLICE * (4 * s + elem), SLICE)
            whole = resid[at, :] + image[:, LANES * elem : LANES * (elem + 1)]
            resid[at, :] = whole
            odd[at, :] = whole * (-1.0 / DIAG)
        if s == 4:
            span_copy(odd, 1).start()
    pack_up[1], pack_down[1] = packed(odd)
    for copy in pitch_copies(1):
        copy.start()

    def interleave(field, rows):
        flat_rows = rows.reshape(125 * SLICES, LANES)
        for j in range(SLICES):
            flat_rows[pl.ds(j, 120, stride=SLICES), :] = field[pl.ds(SLICE * j, 120), :]
            flat_rows[pl.ds(j + 117 * SLICES, 8, stride=SLICES), :] = field[pl.ds(SLICE * j + 117, 8), :]

    interleave(resid, resid_rows)
    rate = OMEGA / DIAG
    for t in range(1, SWEEPS + 1):
        field, after = values[t % 2], values[1 - t % 2]

        def store(j, mine, part):
            at = pl.ds(SLICE * j, SLICE)
            image = (INV_DT + INV_DTAU) * mine + part
            after[at, :] = mine - rate * (resid[at, :] + image)

        apply(field, store)
        correct(after, t, -rate, t < SWEEPS)
    interleave(values[(SWEEPS + 1) % 2], update_rows)


def write_kernel(resid, update, residual_out, update_out, sems):
    copies = [
        pltpu.make_async_copy(rows, out, sems.at[k])
        for k, (rows, out) in enumerate(((update, update_out), (resid, residual_out)))
    ]
    for copy in copies:
        copy.start()
    for copy in copies:
        copy.wait()


def per_device(passes, state, old_state, jacobians, offset):
    shape = state.shape
    tile = TRACE // passes
    in_hbm = pl.BlockSpec(memory_space=pltpu.HBM)
    f32, bf16, dma = jnp.float32, jnp.bfloat16, pltpu.SemaphoreType.DMA
    exchanges = SWEEPS + 1
    viewed = (125, SLICES, 1, LANES)
    pinned = lambda x: pltpu.with_memory_space_constraint(x, pltpu.HBM)
    in_vmem = pl.BlockSpec(memory_space=pltpu.VMEM)
    slices = (SLICE * SLICES + 40, LANES)
    fields = pl.pallas_call(
        functools.partial(kernel, passes),
        out_shape=[jax.ShapeDtypeStruct((625, 4, LANES), f32)] * 2,
        in_specs=[in_hbm, in_hbm, in_hbm, pl.BlockSpec(memory_space=pltpu.SMEM), in_hbm],
        out_specs=[in_vmem] * 2,
        scratch_shapes=[
            pltpu.VMEM(slices, f32),
            pltpu.VMEM(slices, f32),
            pltpu.VMEM(slices, f32),
            pltpu.VMEM((26, SLICES, 1, LANES), f32),
            pltpu.VMEM((passes, tile, LANES), f32),
            pltpu.VMEM((passes, tile, LANES), f32),
            pltpu.VMEM((TRACE + LANES, LANES), f32),
            pltpu.VMEM((13, SLICE, SLICE), f32),
            pltpu.VMEM((3, 8, LANES), f32),
            pltpu.VMEM((5, 3, 5), f32),
            pltpu.VMEM((SLICE + 32, LANES), f32),
            pltpu.VMEM((2 * SLICE, 5 * SLICE), bf16),
            pltpu.VMEM((2 * SLICE, 64), bf16),
            pltpu.VMEM((2 * SLICE, 2 * SLICE), bf16),
            pltpu.VMEM((128, 128), bf16),
            pltpu.VMEM((5, 5 * SLICE, 4 * LANES), bf16),
            pltpu.VMEM((5, 64, 4 * LANES), bf16),
            pltpu.VMEM((exchanges, 32, LANES), f32),
            pltpu.VMEM((exchanges, 32, LANES), f32),
            pltpu.VMEM((exchanges, 32, LANES), f32),
            pltpu.VMEM((exchanges, 32, LANES), f32),
            pltpu.VMEM((exchanges, SLICE, LANES), f32),
            dma((SLICES,)), dma((SLICES,)), dma((5,)), dma, dma,
            pltpu.SemaphoreType.REGULAR, dma, dma, dma, dma, dma((3, exchanges)), dma((3, exchanges)),
        ],
        compiler_params=pltpu.CompilerParams(
            collective_id=0, has_side_effects=True, vmem_limit_bytes=40 * 1024 * 1024
        ),
        name="pseudo_step",
    )(
        pinned(state.reshape(viewed)), pinned(old_state.reshape(viewed)),
        pinned(jnp.transpose(jacobians, (1, 0, 2))), offset, pinned(jnp.asarray(operator_patterns())),
    )
    outs = pl.pallas_call(
        write_kernel,
        out_shape=[jax.ShapeDtypeStruct((625, 4, LANES), f32)] * 2,
        in_specs=[pl.BlockSpec(memory_space=pl.ANY)] * 2,
        out_specs=[in_hbm] * 2,
        scratch_shapes=[dma((2,))],
        compiler_params=pltpu.CompilerParams(vmem_limit_bytes=1024 * 1024),
        name="write_fields",
    )(*fields)
    return tuple(out.reshape(shape) for out in outs)


def solution(mesh):
    placed = P("row", None, None, None, "span", "pass")
    return jax.shard_map(
        functools.partial(per_device, mesh.shape["pass"]),
        mesh=mesh,
        in_specs=(placed, placed, P(), P()),
        out_specs=(placed, placed),
        check_vma=False,
    )
```
